512 devices in a mesh: blk: 64 (over z_lo, y, core), fsdp: 8 (over x, z_hi).
Axes of the slice: x: 4, y: 8, z: 8 (z_hi: 2, z_lo: 4; z = z_hi * 4 + z_lo), core: 2. Of those that a mesh axis runs over, the one named last changes fastest.
Arguments:
- params: float32 [64, 128, 5120], P('blk', 'fsdp'), may hold values from -6.5 to 6.5
- public: float32 [64, 128, 5120], P('blk', 'fsdp'), may hold values from -16 to 16
- mixed: float32 [64, 128, 5120], P('blk', 'fsdp'), may hold values from -16 to 16
- hidden: bfloat16 [64, 2, 1024, 128], P('blk', None, 'fsdp'), may hold values from -6 to 6
- cotangent: bfloat16 [64, 2, 1024, 5120], P('blk', None, 'fsdp'), may hold values from -0.1875 to 0.1875
Outputs:
- new_params: float32 [64, 128, 5120], P('blk', 'fsdp')
- new_public: float32 [64, 128, 5120], P('blk', 'fsdp')
- new_mixed: float32 [64, 128, 5120], P('blk', 'fsdp')
The draws below stay inside these ranges and needn't reach their ends.
All inputs are finite; a program needn't handle non-finite values.
Results may differ from the reference program's by a relative error of at most 0.007.
Values may be sent and summed in bfloat16 or wider, within the bound.
A program may use at most 64 MiB of HBM per device.

```python
import math
import jax
import jax.numpy as jnp
from jax import lax

D = 5120
TOK_DEV = 128
ROUNDS = 2
BLOCK = 32
REPLICAS = 64
ROWS = 128
TOKENS = 1024
N_FSDP = 8


def replica_fields(key, row_low, row_high):
    shared_base = jnp.clip(jax.random.normal(jax.random.fold_in(key, 101), (ROWS, D), jnp.float32), -5.0, 5.0)
    spread = jnp.clip(jax.random.normal(jax.random.fold_in(key, 102), (REPLICAS, ROWS, D), jnp.float32), -5.0, 5.0)
    params = shared_base[None] + 0.3 * spread
    deviation = jnp.clip(jax.random.normal(jax.random.fold_in(key, 103), (REPLICAS, ROWS, D), jnp.float32), -5.0, 5.0)
    row_scale = jnp.exp(jax.random.uniform(jax.random.fold_in(key, 104), (REPLICAS, ROWS, 1), jnp.float32, math.log(row_low), math.log(row_high)))
    col_scale = jnp.exp(jax.random.uniform(jax.random.fold_in(key, 105), (1, 1, D), jnp.float32, math.log(0.5), math.log(1.5)))
    public = params + deviation * row_scale * col_scale
    mixed = (jnp.roll(public, 1, 0) + public + jnp.roll(public, -1, 0)) / 3.0
    return (params, public, mixed)


def draw_params(key, part):
    fields = replica_fields(key, 0.03, 1.0)
    return fields[0]


def draw_public(key, part):
    fields = replica_fields(key, 0.03, 1.0)
    return fields[1]


def draw_mixed(key, part):
    fields = replica_fields(key, 0.03, 1.0)
    return fields[2]


def raised(drawn, stream_key, source, target, parts, factor):
    def block_of(position):
        return (jnp.arange(drawn.shape[position]) // (drawn.shape[position] // parts)).reshape((-1,) + (1,) * (drawn.ndim - 1 - position))

    near = jax.random.permutation(stream_key, parts)[block_of(target)]
    second = (block_of(target) + parts // 2) % parts
    return jnp.where((block_of(source) == near) | (block_of(source) == second), factor * drawn, drawn)


def levels(rng, shape, cuts, low, largest):
    def one(position, parts):
        heights = jax.random.uniform(jax.random.fold_in(jax.random.fold_in(rng, 6), position), (parts,), jnp.float32, low / len(cuts), largest / len(cuts))
        return jnp.repeat(jnp.exp(heights), shape[position] // parts).reshape((-1,) + (1,) * (len(shape) - position - 1))

    loudness = one(*cuts[0])
    for cut in cuts[1:]:
        loudness = loudness * one(*cut)
    return loudness


def gaussian(own_key, dims, scale, limit, cuts=(), dtype=jnp.bfloat16):
    array = jax.random.normal(own_key, dims, jnp.float32) * scale
    if len(cuts) > 0:
        array = levels(own_key, dims, cuts, -0.22, 0.18) * array
    return jnp.clip(array, min=-limit, max=limit).astype(dtype)


def gaussian_with(own_key, shape, width, most, shards, heavy, kind=jnp.bfloat16):
    array = width * jax.random.normal(own_key, shape, jnp.float32)
    if shards:
        array = array * levels(own_key, shape, shards, -0.22, 0.18)
    return jnp.clip(raised(array, jax.random.fold_in(own_key, 3), *heavy), -most, most).astype(kind)


def setup_inputs(seed: int = 0) -> dict:
    key_of = jax.random.split(jax.random.key(seed), 6)
    return {
        "params": draw_params(jax.random.fold_in(key_of[5], 71), 0),
        "public": draw_public(jax.random.fold_in(key_of[5], 71), 0),
        "mixed": draw_mixed(jax.random.fold_in(key_of[5], 71), 0),
        "hidden": gaussian_with(key_of[3], (REPLICAS, ROUNDS, TOKENS, ROWS), 1.0, 6.0, ((0, 64), (2, 8)), (2, 3, 8, 2.0)),
        "cotangent": gaussian(key_of[4], (REPLICAS, ROUNDS, TOKENS, D), TOKENS ** -0.5, 0.1875, ((0, 64), (2, 8))),
    }


LEARN_RATE = 0.25
MIX_RATE = 0.4
SCALE_FLOOR = 0.25
CODE_LIMIT = 2.0

def summed_gradient(activations, cotangents):
    running = jnp.zeros((activations.shape[0], activations.shape[2], cotangents.shape[2]), jnp.float32)
    for group_no in range(N_FSDP):
        act_rows = activations[:, group_no * TOK_DEV:(group_no + 1) * TOK_DEV].astype(jnp.float32)
        cot_rows = cotangents[:, group_no * TOK_DEV:(group_no + 1) * TOK_DEV].astype(jnp.float32)
        partial_sum = jnp.einsum('ntr,ntd->nrd', act_rows, cot_rows).astype(jnp.bfloat16)
        running = running + lax.optimization_barrier(partial_sum).astype(jnp.float32)
    return running

def encode(change):
    blocks = change.reshape(change.shape[0], change.shape[1], change.shape[2] // BLOCK, BLOCK)
    spread = jnp.sqrt(lax.optimization_barrier(jnp.mean(blocks * blocks, axis=3)))
    scales = jnp.maximum(spread, SCALE_FLOOR).astype(jnp.bfloat16)
    wide_scale = jnp.repeat(lax.optimization_barrier(scales).astype(jnp.float32), BLOCK, axis=2)
    encoded = jnp.clip(change / wide_scale, -CODE_LIMIT, CODE_LIMIT).astype(jnp.bfloat16)
    return (encoded, wide_scale)

def reference(params, public, mixed, hidden, cotangent):
    for round_index in range(ROUNDS):
        gradient = summed_gradient(hidden[:, round_index], cotangent[:, round_index])
        stepped = params - LEARN_RATE * gradient
        encoded, wide_scale = encode(stepped - public)
        message = encoded.astype(jnp.float32) * wide_scale
        public = public + message
        mixed = mixed + (message + jnp.roll(message, 1, 0) + jnp.roll(message, -1, 0)) / 3.0
        params = stepped + MIX_RATE * (mixed - public)
    return (params, public, mixed)
```

```python
import functools

import jax
import jax.numpy as jnp
from jax import lax
from jax.experimental import pallas as pl
from jax.experimental.pallas import tpu as pltpu
from jax.sharding import PartitionSpec as P

MESH = pl.DeviceIdType.MESH
BLOCK = 32
LANES = 128
LEARN_RATE = 0.25
MIX_RATE = 0.4
SCALE_FLOOR = 0.25
CODE_LIMIT = 2.0
CHUNKS = 5
XSIDE = 4
AHEAD = 3
LAGS = (2, 4, 6)

TO_RIGHT, TO_LEFT, SUM_O, SUM_M, OVER, GO_AFTER, GO_BEFORE = range(7)
PARTS, SUMS, ACROSS, GOSSIP = range(4)
LANDS = ((0, 4), (4, 2), (6, 1), (7, 2))
INBOX = 9
NEAR_M, FAR_O, FAR_M, NEAR_O, IN_SUM_O, IN_SUM_M, IN_ACROSS, IN_BEFORE, IN_AFTER = range(INBOX)

OWN_MINE, NEXT_OTHER, LAST_MINE, OWN_OTHER = 0, 1, 2, 3
LEFT_PAIR, RIGHT_PAIR = 4, 6


def tall(wide):
    n = wide.shape[1] // LANES
    return jnp.concatenate([wide[:, i * LANES:(i + 1) * LANES] for i in range(n)], axis=0)


def flat(high, rows):
    n = high.shape[0] // rows
    return jnp.concatenate([high[i * rows:(i + 1) * rows] for i in range(n)], axis=1)


def add(*refs):
    total = refs[0][...].astype(jnp.float32)
    for ref in refs[1:]:
        total = total + ref[...].astype(jnp.float32)
    return total


def kernel(par_hbm, pub_hbm, mix_hbm, hid_hbm, cot_hbm, opar, opub, omix,
           hid, hid_t, cot, par, pub, mix, part, inbox, fwd_o, fwd_m, zout, gout, step_v, mess_v, pool,
           hid_sem, cot_sem, state_sem, send_sem, recv_sem):
    rounds, tokens, rows_all = hid.shape
    chunks, rows, w = par.shape
    items = rounds * chunks

    b = lax.axis_index("blk")
    f = lax.axis_index("fsdp")
    nb = lax.axis_size("blk")
    x, zh = f // 2, f % 2
    right = (b, (x + 1) % XSIDE * 2 + zh)
    left = (b, (x + XSIDE - 1) % XSIDE * 2 + zh)
    across = (b, x * 2 + 1 - zh)
    after = ((b + 1) % nb, f)
    before = ((b + nb - 1) % nb, f)

    barrier = pltpu.get_barrier_semaphore()
    for device in (right, left, across, after, before):
        pl.semaphore_signal(barrier, inc=1, device_id=device, device_id_type=MESH)

    def cols(c):
        return pl.ds(pl.multiple_of(c * w, LANES), w)

    hid_load = pltpu.make_async_copy(hid_hbm.at[0], hid, hid_sem.at[0])

    def cot_load(t):
        return pltpu.make_async_copy(cot_hbm.at[0, t // chunks, :, cols(t % chunks)], cot.at[t], cot_sem.at[t])

    def state_loads(c):
        return [pltpu.make_async_copy(src.at[0, :, cols(c)], dst.at[c], state_sem.at[i, c])
                for i, (src, dst) in enumerate(((par_hbm, par), (pub_hbm, pub), (mix_hbm, mix)))]

    hid_load.start()
    for t in range(AHEAD):
        cot_load(t).start()

    @pl.loop(AHEAD, items)
    def _(t):
        cot_load(t).start()

    @pl.loop(0, chunks)
    def _(c):
        for copy in state_loads(c):
            copy.start()

    def land(t, first, blocks=1):
        return inbox.at[t, pl.ds(first, blocks)]

    def start(kind, t):
        src, dst, device, group = {
            TO_RIGHT: lambda: (part.at[t, pl.ds(RIGHT_PAIR, 2)], land(t, NEAR_M, 2), right, PARTS),
            TO_LEFT: lambda: (part.at[t, pl.ds(LEFT_PAIR, 2)], land(t, FAR_M, 2), left, PARTS),
            SUM_O: lambda: (fwd_o.at[pl.ds(t, 1)], land(t, IN_SUM_O), right, SUMS),
            SUM_M: lambda: (fwd_m.at[pl.ds(t, 1)], land(t, IN_SUM_M), left, SUMS),
            OVER: lambda: (zout.at[pl.ds(t, 1)], land(t, IN_ACROSS), across, ACROSS),
            GO_AFTER: lambda: (gout.at[pl.ds(t, 1)], land(t, IN_BEFORE), after, GOSSIP),
            GO_BEFORE: lambda: (gout.at[pl.ds(t, 1)], land(t, IN_AFTER), before, GOSSIP),
        }[kind]()
        pltpu.make_async_remote_copy(
            src_ref=src, dst_ref=dst, send_sem=send_sem.at[0], recv_sem=recv_sem.at[group, t],
            device_id=device, device_id_type=MESH).start()

    def arrived(group, t):
        blocks = land(t, *LANDS[group])
        pltpu.make_async_copy(blocks, blocks, recv_sem.at[group, t]).wait()

    places = [3 * ((j // 2 + XSIDE - x) % XSIDE * 2 + (j + zh) % 2) % 8 for j in range(rows_all // rows)]

    def multiply(t):
        cot_load(t).wait()
        product = jnp.dot(hid_t[t // chunks], cot[t], preferred_element_type=jnp.float32).astype(jnp.bfloat16)
        for j, place in enumerate(places):
            part[t, place] = product[j * rows:(j + 1) * rows]

    def send_parts(t):
        start(TO_RIGHT, t)
        start(TO_LEFT, t)

    def pass_on(t):
        arrived(PARTS, t)
        fwd_o[t] = add(inbox.at[t, FAR_O], part.at[t, NEXT_OTHER]).astype(jnp.bfloat16)
        start(SUM_O, t)
        fwd_m[t] = add(inbox.at[t, FAR_M], part.at[t, LAST_MINE]).astype(jnp.bfloat16)
        start(SUM_M, t)

    def over_z(t):
        arrived(SUMS, t)
        zout[t] = add(part.at[t, OWN_OTHER], inbox.at[t, NEAR_O], inbox.at[t, IN_SUM_O]).astype(jnp.bfloat16)
        start(OVER, t)

    def encode(t):
        c = t % chunks

        @pl.when(t < chunks)
        def _():
            for copy in state_loads(c):
                copy.wait()

        arrived(ACROSS, t)
        gradient = add(part.at[t, OWN_MINE], inbox.at[t, NEAR_M], inbox.at[t, IN_SUM_M], inbox.at[t, IN_ACROSS])
        stepped = par[c] - LEARN_RATE * gradient
        public = pub[c]
        change = tall(stepped - public)
        square = change * change
        high = square.astype(jnp.bfloat16)
        low = (square - high.astype(jnp.float32)).astype(jnp.bfloat16)
        energy = jnp.dot(jnp.concatenate([high, low], axis=1), pool[...], preferred_element_type=jnp.float32)
        scales = jnp.maximum(jnp.sqrt(energy * (1.0 / BLOCK)), SCALE_FLOOR).astype(jnp.bfloat16)
        wide = scales.astype(jnp.float32)
        coded = jnp.clip(change / wide, -CODE_LIMIT, CODE_LIMIT).astype(jnp.bfloat16)
        message = flat(coded.astype(jnp.float32) * wide, rows)
        gout[t] = message.astype(jnp.bfloat16)
        start(GO_AFTER, t)
        start(GO_BEFORE, t)
        pub[c] = public + message
        step_v[c] = stepped
        mess_v[c] = message

    def update(t):
        c = t % chunks
        arrived(GOSSIP, t)
        public = pub[c]
        heard = mess_v[c] + add(inbox.at[t, IN_BEFORE], inbox.at[t, IN_AFTER])
        mixed = mix[c] + heard * (1.0 / 3.0)
        params = step_v[c] + MIX_RATE * (mixed - public)

        @pl.when(t < items - chunks)
        def _():
            mix[c] = mixed
            par[c] = params

        @pl.when(t >= items - chunks)
        def _():
            opar[0, :, cols(c)] = params
            opub[0, :, cols(c)] = public
            omix[0, :, cols(c)] = mixed

    block = lax.broadcasted_iota(jnp.int32, pool.shape, 0) % LANES // BLOCK
    lane_block = lax.broadcasted_iota(jnp.int32, pool.shape, 1) // BLOCK

    hid_load.wait()
    hid_t[0] = hid[0].T
    multiply(0)
    pl.semaphore_wait(barrier, 5)
    send_parts(0)
    for t in range(1, AHEAD):
        multiply(t)
        send_parts(t)
    for r in range(1, rounds):
        hid_t[r] = hid[r].T
    pool[...] = (block == lane_block).astype(jnp.bfloat16)

    @pl.loop(AHEAD, items)
    def _(t):
        multiply(t)

    def stage(work, item):
        @pl.when((item >= 0) & (item < items))
        def _():
            work(item)

    @pl.loop(0, items + LAGS[-1])
    def _(t):
        stage(pass_on, t)
        stage(send_parts, t + AHEAD)
        for work, lag in zip((over_z, encode, update), LAGS):
            stage(work, t - lag)

    pltpu.make_async_copy(inbox, inbox, send_sem.at[0]).wait()


def deliver(*refs):
    sem = refs[-1]
    arrays = (len(refs) - 1) // 2
    copies = []
    for i in range(arrays):
        half = refs[i].shape[1] // 2
        for j in range(2):
            piece = (0, pl.ds(j * half, half))
            copies.append(pltpu.make_async_copy(refs[i].at[piece], refs[arrays + i].at[piece], sem.at[i, j]))
    for copy in copies:
        copy.start()
    for copy in copies:
        copy.wait()


def per_device(params, public, mixed, hidden, cotangent):
    _, rows, width = params.shape
    _, rounds, tokens, rows_all = hidden.shape
    items = rounds * CHUNKS
    w = width // CHUNKS
    piece = pltpu.VMEM((items, rows, w), jnp.bfloat16)
    state = pltpu.VMEM((CHUNKS, rows, w), jnp.float32)
    anywhere = pl.BlockSpec(memory_space=pl.ANY)
    in_vmem = pl.BlockSpec(memory_space=pltpu.VMEM)
    results = pl.pallas_call(
        kernel,
        out_shape=(pltpu.VMEM(params.shape, jnp.float32),) * 3,
        in_specs=[anywhere] * 5,
        out_specs=(in_vmem,) * 3,
        scratch_shapes=[
            pltpu.VMEM((rounds, tokens, rows_all), jnp.bfloat16),
            pltpu.VMEM((rounds, rows_all, tokens), jnp.bfloat16),
            pltpu.VMEM((items, tokens, w), jnp.bfloat16),
            state, state, state,
            pltpu.VMEM((items, rows_all // rows, rows, w), jnp.bfloat16),
            pltpu.VMEM((items, INBOX, rows, w), jnp.bfloat16),
            *[piece] * 4,
            state, state,
            pltpu.VMEM((2 * LANES, LANES), jnp.bfloat16),
            pltpu.SemaphoreType.DMA((1,)),
            pltpu.SemaphoreType.DMA((items,)),
            pltpu.SemaphoreType.DMA((3, CHUNKS)),
            pltpu.SemaphoreType.DMA((1,)),
            pltpu.SemaphoreType.DMA((len(LANDS), items)),
        ],
        compiler_params=pltpu.CompilerParams(
            collective_id=0, has_side_effects=True, vmem_limit_bytes=40 * 1024 * 1024),
        cost_estimate=pl.CostEstimate(flops=340_000_000, bytes_accessed=5_000_000, transcendentals=0),
    )(*[pltpu.with_memory_space_constraint(a, pltpu.HBM) for a in (params, public, mixed, hidden, cotangent)])
    return pl.pallas_call(
        deliver,
        out_shape=(jax.ShapeDtypeStruct(params.shape, jnp.float32),) * 3,
        in_specs=[in_vmem] * 3,
        out_specs=(anywhere,) * 3,
        scratch_shapes=[pltpu.SemaphoreType.DMA((3, 2))],
        compiler_params=pltpu.CompilerParams(vmem_limit_bytes=1024 * 1024),
    )(*[pltpu.with_memory_space_constraint(a, pltpu.VMEM) for a in results])


def solution(mesh):
    state = P("blk", "fsdp", None)
    tokens = P("blk", None, "fsdp", None)
    return jax.shard_map(
        per_device,
        mesh=mesh,
        in_specs=(state, state, state, tokens, tokens),
        out_specs=(state, state, state),
        check_vma=False,
    )
```

```python
import functools

import jax
import jax.numpy as jnp
from jax import lax
from jax.experimental import pallas as pl
from jax.experimental.pallas import tpu as pltpu
from jax.sharding import PartitionSpec as P

MESH = pl.DeviceIdType.MESH
BLOCK = 32
LANES = 128
LEARN_RATE = 0.25
MIX_RATE = 0.4
SCALE_FLOOR = 0.25
CODE_LIMIT = 2.0
CHUNKS = 5
XSIDE = 4
AHEAD = 3
LAGS = (2, 4, 6)

TO_RIGHT, TO_LEFT, SUM_O, SUM_M, OVER, GO_AFTER, GO_BEFORE = range(7)
PARTS, SUMS, ACROSS, GOSSIP = range(4)
LANDS = ((0, 4), (4, 2), (6, 1), (7, 2))
INBOX = 9
NEAR_M, FAR_O, FAR_M, NEAR_O, IN_SUM_O, IN_SUM_M, IN_ACROSS, IN_BEFORE, IN_AFTER = range(INBOX)

PIECES = 2
LANDS_LAST = {PARTS: (0, 6), ACROSS: (6, 1), GOSSIP: (7, 2)}

OWN_MINE, NEXT_OTHER, LAST_MINE, OWN_OTHER = 0, 1, 2, 3
LEFT_PAIR, RIGHT_PAIR = 4, 6


def tall(wide):
    n = wide.shape[1] // LANES
    return jnp.concatenate([wide[:, i * LANES:(i + 1) * LANES] for i in range(n)], axis=0)


def flat(high, rows):
    n = high.shape[0] // rows
    return jnp.concatenate([high[i * rows:(i + 1) * rows] for i in range(n)], axis=1)


def add(*refs):
    total = refs[0][...].astype(jnp.float32)
    for ref in refs[1:]:
        total = total + ref[...].astype(jnp.float32)
    return total


def kernel(par_hbm, pub_hbm, mix_hbm, hid_hbm, cot_hbm, opar, opub, omix,
           hid, hid_t, cot, par, pub, mix, part, inbox, fwd_o, fwd_m, zout, gout, step_v, mess_v, pool,
           last_part, last_inbox, last_zout, last_gout,
           hid_sem, cot_sem, state_sem, send_sem, recv_sem, last_recv_sem):
    rounds, tokens, rows_all = hid.shape
    chunks, rows, w = par.shape
    items = rounds * chunks - 1
    wl = w // PIECES

    b = lax.axis_index("blk")
    f = lax.axis_index("fsdp")
    nb = lax.axis_size("blk")
    x, zh = f // 2, f % 2
    right = (b, (x + 1) % XSIDE * 2 + zh)
    left = (b, (x + XSIDE - 1) % XSIDE * 2 + zh)
    across = (b, x * 2 + 1 - zh)
    opposite = (b, (x + 2) % XSIDE * 2 + zh)
    after = ((b + 1) % nb, f)
    before = ((b + nb - 1) % nb, f)

    barrier = pltpu.get_barrier_semaphore()
    for device in (right, left, opposite, across, after, before):
        pl.semaphore_signal(barrier, inc=1, device_id=device, device_id_type=MESH)

    def cols(c):
        return pl.ds(pl.multiple_of(c * w, LANES), w)

    hid_load = pltpu.make_async_copy(hid_hbm.at[0], hid, hid_sem.at[0])

    def cot_load(t):
        return pltpu.make_async_copy(cot_hbm.at[0, t // chunks, :, cols(t % chunks)], cot.at[t], cot_sem.at[t])

    def state_loads(c):
        return [pltpu.make_async_copy(src.at[0, :, cols(c)], dst.at[c], state_sem.at[i, c])
                for i, (src, dst) in enumerate(((par_hbm, par), (pub_hbm, pub), (mix_hbm, mix)))]

    hid_load.start()
    for t in range(AHEAD):
        cot_load(t).start()

    def land(t, first, blocks=1):
        return inbox.at[t, pl.ds(first, blocks)]

    def start(kind, t):
        src, dst, device, group = {
            TO_RIGHT: lambda: (part.at[t, pl.ds(RIGHT_PAIR, 2)], land(t, NEAR_M, 2), right, PARTS),
            TO_LEFT: lambda: (part.at[t, pl.ds(LEFT_PAIR, 2)], land(t, FAR_M, 2), left, PARTS),
            SUM_O: lambda: (fwd_o.at[pl.ds(t, 1)], land(t, IN_SUM_O), right, SUMS),
            SUM_M: lambda: (fwd_m.at[pl.ds(t, 1)], land(t, IN_SUM_M), left, SUMS),
            OVER: lambda: (zout.at[pl.ds(t, 1)], land(t, IN_ACROSS), across, ACROSS),
            GO_AFTER: lambda: (gout.at[pl.ds(t, 1)], land(t, IN_BEFORE), after, GOSSIP),
            GO_BEFORE: lambda: (gout.at[pl.ds(t, 1)], land(t, IN_AFTER), before, GOSSIP),
        }[kind]()
        pltpu.make_async_remote_copy(
            src_ref=src, dst_ref=dst, send_sem=send_sem.at[0], recv_sem=recv_sem.at[group, t],
            device_id=device, device_id_type=MESH).start()

    def arrived(group, t):
        blocks = land(t, *LANDS[group])
        pltpu.make_async_copy(blocks, blocks, recv_sem.at[group, t]).wait()

    places = [3 * ((j // 2 + XSIDE - x) % XSIDE * 2 + (j + zh) % 2) % 8 for j in range(rows_all // rows)]

    def product(t):
        cot_load(t).wait()
        return jnp.dot(hid_t[t // chunks], cot[t], preferred_element_type=jnp.float32).astype(jnp.bfloat16)

    def multiply(t):
        blocks = product(t)
        for j, place in enumerate(places):
            part[t, place] = blocks[j * rows:(j + 1) * rows]

    def multiply_last():
        blocks = product(items)
        for j, place in enumerate(places):
            for k in range(PIECES):
                last_part[k, place * 3 % 8] = blocks[j * rows:(j + 1) * rows, k * wl:(k + 1) * wl]

    def send_parts(t):
        start(TO_RIGHT, t)
        start(TO_LEFT, t)

    def pass_on(t):
        arrived(PARTS, t)
        fwd_o[t] = add(inbox.at[t, FAR_O], part.at[t, NEXT_OTHER]).astype(jnp.bfloat16)
        start(SUM_O, t)
        fwd_m[t] = add(inbox.at[t, FAR_M], part.at[t, LAST_MINE]).astype(jnp.bfloat16)
        start(SUM_M, t)

    def over_z(t):
        arrived(SUMS, t)
        zout[t] = add(part.at[t, OWN_OTHER], inbox.at[t, NEAR_O], inbox.at[t, IN_SUM_O]).astype(jnp.bfloat16)
        start(OVER, t)

    def code(c, columns, gradient):
        stepped = par[c, :, columns] - LEARN_RATE * gradient
        public = pub[c, :, columns]
        change = tall(stepped - public)
        square = change * change
        high = square.astype(jnp.bfloat16)
        low = (square - high.astype(jnp.float32)).astype(jnp.bfloat16)
        energy = jnp.dot(jnp.concatenate([high, low], axis=1), pool[...], preferred_element_type=jnp.float32)
        scales = jnp.maximum(jnp.sqrt(energy * (1.0 / BLOCK)), SCALE_FLOOR).astype(jnp.bfloat16)
        wide = scales.astype(jnp.float32)
        coded = jnp.clip(change / wide, -CODE_LIMIT, CODE_LIMIT).astype(jnp.bfloat16)
        message = flat(coded.astype(jnp.float32) * wide, rows)
        pub[c, :, columns] = public + message
        step_v[c, :, columns] = stepped
        mess_v[c, :, columns] = message
        return message.astype(jnp.bfloat16)

    def mix_in(c, columns, heard):
        public = pub[c, :, columns]
        mixed = mix[c, :, columns] + (mess_v[c, :, columns] + heard) * (1.0 / 3.0)
        return step_v[c, :, columns] + MIX_RATE * (mixed - public), public, mixed

    def encode(t):
        c = t % chunks

        @pl.when(t < chunks)
        def _():
            for copy in state_loads(c):
                copy.wait()

        arrived(ACROSS, t)
        gradient = add(part.at[t, OWN_MINE], inbox.at[t, NEAR_M], inbox.at[t, IN_SUM_M], inbox.at[t, IN_ACROSS])
        gout[t] = code(c, slice(0, w), gradient)
        start(GO_AFTER, t)
        start(GO_BEFORE, t)

    def update(t):
        c = t % chunks
        arrived(GOSSIP, t)
        params, public, mixed = mix_in(c, slice(0, w), add(inbox.at[t, IN_BEFORE], inbox.at[t, IN_AFTER]))

        @pl.when(t < (rounds - 1) * chunks)
        def _():
            mix[c] = mixed
            par[c] = params

        @pl.when(t >= (rounds - 1) * chunks)
        def _():
            opar[0, :, cols(c)] = params
            opub[0, :, cols(c)] = public
            omix[0, :, cols(c)] = mixed

    def last_start(k, src, slot, device, group):
        pltpu.make_async_remote_copy(
            src_ref=src, dst_ref=last_inbox.at[k, pl.ds(slot, src.shape[0])], send_sem=send_sem.at[1],
            recv_sem=last_recv_sem.at[group, k], device_id=device, device_id_type=MESH).start()

    def last_arrived(group, k):
        first, blocks = LANDS_LAST[group]
        blocks = last_inbox.at[k, pl.ds(first, blocks)]
        pltpu.make_async_copy(blocks, blocks, last_recv_sem.at[group, k]).wait()

    def last_send_parts(k):
        for d, device in ((2, opposite), (1, right), (3, left)):
            last_start(k, last_part.at[k, pl.ds(2 * d, 2)], 2 * d - 2, device, PARTS)

    def last_over_z(k):
        last_arrived(PARTS, k)
        last_zout[k] = add(*[last_part.at[k, 1]] + [last_inbox.at[k, i] for i in (1, 3, 5)]).astype(jnp.bfloat16)
        last_start(k, last_zout.at[pl.ds(k, 1)], LANDS_LAST[ACROSS][0], across, ACROSS)

    def last_encode(k):
        last_arrived(ACROSS, k)
        gradient = add(*[last_part.at[k, 0]] + [last_inbox.at[k, i] for i in (0, 2, 4, 6)])
        last_gout[k] = code(chunks - 1, slice(k * wl, (k + 1) * wl), gradient)
        first = LANDS_LAST[GOSSIP][0]
        last_start(k, last_gout.at[pl.ds(k, 1)], first, after, GOSSIP)
        last_start(k, last_gout.at[pl.ds(k, 1)], first + 1, before, GOSSIP)

    def last_update(k):
        last_arrived(GOSSIP, k)
        columns = slice(k * wl, (k + 1) * wl)
        first = LANDS_LAST[GOSSIP][0]
        params, public, mixed = mix_in(chunks - 1, columns, add(last_inbox.at[k, first], last_inbox.at[k, first + 1]))
        there = pl.ds((chunks - 1) * w + k * wl, wl)
        opar[0, :, there] = params
        opub[0, :, there] = public
        omix[0, :, there] = mixed

    block = lax.broadcasted_iota(jnp.int32, pool.shape, 0) % LANES // BLOCK
    lane_block = lax.broadcasted_iota(jnp.int32, pool.shape, 1) // BLOCK

    hid_load.wait()
    hid_t[0] = hid[0].T
    multiply(0)
    pl.semaphore_wait(barrier, 6)
    send_parts(0)

    @pl.loop(AHEAD, items + 1)
    def _(t):
        cot_load(t).start()

    @pl.loop(0, chunks)
    def _(c):
        for copy in state_loads(c):
            copy.start()

    for t in range(1, AHEAD):
        multiply(t)
        send_parts(t)
    for r in range(1, rounds):
        hid_t[r] = hid[r].T
    pool[...] = (block == lane_block).astype(jnp.bfloat16)

    @pl.loop(AHEAD, items)
    def _(t):
        multiply(t)

    multiply_last()

    def stage(work, item):
        @pl.when((item >= 0) & (item < items))
        def _():
            work(item)

    late = {items - 2: ((last_send_parts, 0),), items - 1: ((last_send_parts, 1),),
            items: ((last_over_z, 0),), items + 1: ((last_over_z, 1),),
            items + 2: ((last_encode, 0),), items + 3: ((last_encode, 1),),
            items + 5: ((last_update, 0), (last_update, 1))}

    @pl.loop(0, items + LAGS[-1])
    def _(t):
        stage(pass_on, t)
        stage(send_parts, t + AHEAD)
        for work, lag in zip((over_z, encode, update), LAGS):
            stage(work, t - lag)
        for step, works in late.items():
            @pl.when(t == step)
            def _():
                for work, k in works:
                    work(k)

    pltpu.make_async_copy(inbox, inbox, send_sem.at[0]).wait()
    pltpu.make_async_copy(last_inbox, last_inbox, send_sem.at[1]).wait()


def deliver(*refs):
    sem = refs[-1]
    arrays = (len(refs) - 1) // 2
    copies = []
    for i in range(arrays):
        half = refs[i].shape[1] // 2
        for j in range(2):
            piece = (0, pl.ds(j * half, half))
            copies.append(pltpu.make_async_copy(refs[i].at[piece], refs[arrays + i].at[piece], sem.at[i, j]))
    for copy in copies:
        copy.start()
    for copy in copies:
        copy.wait()


def per_device(params, public, mixed, hidden, cotangent):
    _, rows, width = params.shape
    _, rounds, tokens, rows_all = hidden.shape
    items = rounds * CHUNKS - 1
    w = width // CHUNKS
    piece = pltpu.VMEM((items, rows, w), jnp.bfloat16)
    state = pltpu.VMEM((CHUNKS, rows, w), jnp.float32)
    anywhere = pl.BlockSpec(memory_space=pl.ANY)
    in_vmem = pl.BlockSpec(memory_space=pltpu.VMEM)
    results = pl.pallas_call(
        kernel,
        out_shape=(pltpu.VMEM(params.shape, jnp.float32),) * 3,
        in_specs=[anywhere] * 5,
        out_specs=(in_vmem,) * 3,
        scratch_shapes=[
            pltpu.VMEM((rounds, tokens, rows_all), jnp.bfloat16),
            pltpu.VMEM((rounds, rows_all, tokens), jnp.bfloat16),
            pltpu.VMEM((items + 1, tokens, w), jnp.bfloat16),
            state, state, state,
            pltpu.VMEM((items, rows_all // rows, rows, w), jnp.bfloat16),
            pltpu.VMEM((items, INBOX, rows, w), jnp.bfloat16),
            *[piece] * 4,
            state, state,
            pltpu.VMEM((2 * LANES, LANES), jnp.bfloat16),
            pltpu.VMEM((PIECES, rows_all // rows, rows, w // PIECES), jnp.bfloat16),
            pltpu.VMEM((PIECES, INBOX, rows, w // PIECES), jnp.bfloat16),
            pltpu.VMEM((PIECES, rows, w // PIECES), jnp.bfloat16),
            pltpu.VMEM((PIECES, rows, w // PIECES), jnp.bfloat16),
            pltpu.SemaphoreType.DMA((1,)),
            pltpu.SemaphoreType.DMA((items + 1,)),
            pltpu.SemaphoreType.DMA((3, CHUNKS)),
            pltpu.SemaphoreType.DMA((2,)),
            pltpu.SemaphoreType.DMA((len(LANDS), items)),
            pltpu.SemaphoreType.DMA((len(LANDS), PIECES)),
        ],
        compiler_params=pltpu.CompilerParams(
            collective_id=0, has_side_effects=True, vmem_limit_bytes=40 * 1024 * 1024),
        cost_estimate=pl.CostEstimate(flops=340_000_000, bytes_accessed=5_000_000, transcendentals=0),
    )(*[pltpu.with_memory_space_constraint(a, pltpu.HBM) for a in (params, public, mixed, hidden, cotangent)])
    return pl.pallas_call(
        deliver,
        out_shape=(jax.ShapeDtypeStruct(params.shape, jnp.float32),) * 3,
        in_specs=[in_vmem] * 3,
        out_specs=(anywhere,) * 3,
        scratch_shapes=[pltpu.SemaphoreType.DMA((3, 2))],
        compiler_params=pltpu.CompilerParams(vmem_limit_bytes=1024 * 1024),
    )(*[pltpu.with_memory_space_constraint(a, pltpu.VMEM) for a in results])


def solution(mesh):
    state = P("blk", "fsdp", None)
    tokens = P("blk", None, "fsdp", None)
    return jax.shard_map(
        per_device,
        mesh=mesh,
        in_specs=(state, state, state, tokens, tokens),
        out_specs=(state, state, state),
        check_vma=False,
    )
```

```python
import functools

import jax
import jax.numpy as jnp
from jax import lax
from jax.experimental import pallas as pl
from jax.experimental.pallas import tpu as pltpu
from jax.sharding import PartitionSpec as P

MESH = pl.DeviceIdType.MESH
BLOCK = 32
LANES = 128
LEARN_RATE = 0.25
MIX_RATE = 0.4
SCALE_FLOOR = 0.25
CODE_LIMIT = 2.0
CHUNKS = 4
XSIDE = 4
AHEAD = 3
LAGS = (2, 4, 6)

TO_RIGHT, TO_LEFT, SUM_O, SUM_M, OVER, GO_AFTER, GO_BEFORE = range(7)
PARTS, SUMS, ACROSS, GOSSIP = range(4)
LANDS = ((0, 4), (4, 2), (6, 1), (7, 2))
INBOX = 9
NEAR_M, FAR_O, FAR_M, NEAR_O, IN_SUM_O, IN_SUM_M, IN_ACROSS, IN_BEFORE, IN_AFTER = range(INBOX)

PIECES = 4
LANDS_X_FIRST = {PARTS: (0, 6), ACROSS: (6, 1), GOSSIP: (7, 2)}
LANDS_Z_FIRST = {ACROSS: (0, 4), PARTS: (4, 3), GOSSIP: (7, 2)}

OWN_MINE, NEXT_OTHER, LAST_MINE, OWN_OTHER = 0, 1, 2, 3
LEFT_PAIR, RIGHT_PAIR = 4, 6


def tall(wide):
    n = wide.shape[1] // LANES
    return jnp.concatenate([wide[:, i * LANES:(i + 1) * LANES] for i in range(n)], axis=0)


def flat(high, rows):
    n = high.shape[0] // rows
    return jnp.concatenate([high[i * rows:(i + 1) * rows] for i in range(n)], axis=1)


def add(*refs):
    total = refs[0][...].astype(jnp.float32)
    for ref in refs[1:]:
        total = total + ref[...].astype(jnp.float32)
    return total


def kernel(par_hbm, pub_hbm, mix_hbm, hid_hbm, cot_hbm, opar, opub, omix,
           hid, hid_t, cot, par, pub, mix, part, inbox, fwd_o, fwd_m, zout, gout, step_v, mess_v, pool,
           last_part, last_inbox, last_zout, last_sums, last_gout,
           hid_sem, cot_sem, state_sem, send_sem, recv_sem, last_recv_sem):
    rounds, tokens, rows_all = hid.shape
    chunks, rows, w = par.shape
    items = rounds * chunks - 2
    wl = w // 2

    b = lax.axis_index("blk")
    f = lax.axis_index("fsdp")
    nb = lax.axis_size("blk")
    x, zh = f // 2, f % 2
    right = (b, (x + 1) % XSIDE * 2 + zh)
    left = (b, (x + XSIDE - 1) % XSIDE * 2 + zh)
    across = (b, x * 2 + 1 - zh)
    opposite = (b, (x + 2) % XSIDE * 2 + zh)
    after = ((b + 1) % nb, f)
    before = ((b + nb - 1) % nb, f)

    barrier = pltpu.get_barrier_semaphore()
    for device in (right, left, opposite, across, after, before):
        pl.semaphore_signal(barrier, inc=1, device_id=device, device_id_type=MESH)

    def cols(c):
        return pl.ds(pl.multiple_of(c * w, LANES), w)

    hid_load = pltpu.make_async_copy(hid_hbm.at[0], hid, hid_sem.at[0])

    def cot_load(t):
        return pltpu.make_async_copy(cot_hbm.at[0, t // chunks, :, cols(t % chunks)], cot.at[t], cot_sem.at[t])

    def state_loads(c):
        return [pltpu.make_async_copy(src.at[0, :, cols(c)], dst.at[c], state_sem.at[i, c])
                for i, (src, dst) in enumerate(((par_hbm, par), (pub_hbm, pub), (mix_hbm, mix)))]

    hid_load.start()
    for t in range(AHEAD):
        cot_load(t).start()

    def land(t, first, blocks=1):
        return inbox.at[t, pl.ds(first, blocks)]

    def start(kind, t):
        src, dst, device, group = {
            TO_RIGHT: lambda: (part.at[t, pl.ds(RIGHT_PAIR, 2)], land(t, NEAR_M, 2), right, PARTS),
            TO_LEFT: lambda: (part.at[t, pl.ds(LEFT_PAIR, 2)], land(t, FAR_M, 2), left, PARTS),
            SUM_O: lambda: (fwd_o.at[pl.ds(t, 1)], land(t, IN_SUM_O), right, SUMS),
            SUM_M: lambda: (fwd_m.at[pl.ds(t, 1)], land(t, IN_SUM_M), left, SUMS),
            OVER: lambda: (zout.at[pl.ds(t, 1)], land(t, IN_ACROSS), across, ACROSS),
            GO_AFTER: lambda: (gout.at[pl.ds(t, 1)], land(t, IN_BEFORE), after, GOSSIP),
            GO_BEFORE: lambda: (gout.at[pl.ds(t, 1)], land(t, IN_AFTER), before, GOSSIP),
        }[kind]()
        pltpu.make_async_remote_copy(
            src_ref=src, dst_ref=dst, send_sem=send_sem.at[0], recv_sem=recv_sem.at[group, t],
            device_id=device, device_id_type=MESH).start()

    def arrived(group, t):
        blocks = land(t, *LANDS[group])
        pltpu.make_async_copy(blocks, blocks, recv_sem.at[group, t]).wait()

    places = [3 * ((j // 2 + XSIDE - x) % XSIDE * 2 + (j + zh) % 2) % 8 for j in range(rows_all // rows)]

    def product(t):
        cot_load(t).wait()
        return jnp.dot(hid_t[t // chunks], cot[t], preferred_element_type=jnp.float32).astype(jnp.bfloat16)

    def multiply(t):
        blocks = product(t)
        for j, place in enumerate(places):
            part[t, place] = blocks[j * rows:(j + 1) * rows]

    def multiply_last(pair):
        blocks = product(items + pair)
        for j, place in enumerate(places):
            which = place * 3 % 8
            if pair == 1:
                which = which % 2 * XSIDE + which // 2
            for i in range(2):
                last_part[2 * pair + i, which] = blocks[j * rows:(j + 1) * rows, i * wl:(i + 1) * wl]

    def send_parts(t):
        start(TO_RIGHT, t)
        start(TO_LEFT, t)

    def pass_on(t):
        arrived(PARTS, t)
        fwd_o[t] = add(inbox.at[t, FAR_O], part.at[t, NEXT_OTHER]).astype(jnp.bfloat16)
        start(SUM_O, t)
        fwd_m[t] = add(inbox.at[t, FAR_M], part.at[t, LAST_MINE]).astype(jnp.bfloat16)
        start(SUM_M, t)

    def over_z(t):
        arrived(SUMS, t)
        zout[t] = add(part.at[t, OWN_OTHER], inbox.at[t, NEAR_O], inbox.at[t, IN_SUM_O]).astype(jnp.bfloat16)
        start(OVER, t)

    def code(c, columns, gradient):
        stepped = par[c, :, columns] - LEARN_RATE * gradient
        public = pub[c, :, columns]
        change = tall(stepped - public)
        square = change * change
        high = square.astype(jnp.bfloat16)
        low = (square - high.astype(jnp.float32)).astype(jnp.bfloat16)
        energy = jnp.dot(jnp.concatenate([high, low], axis=1), pool[...], preferred_element_type=jnp.float32)
        scales = jnp.maximum(jnp.sqrt(energy * (1.0 / BLOCK)), SCALE_FLOOR).astype(jnp.bfloat16)
        wide = scales.astype(jnp.float32)
        coded = jnp.clip(change / wide, -CODE_LIMIT, CODE_LIMIT).astype(jnp.bfloat16)
        message = flat(coded.astype(jnp.float32) * wide, rows)
        pub[c, :, columns] = public + message
        step_v[c, :, columns] = stepped
        mess_v[c, :, columns] = message
        return message.astype(jnp.bfloat16)

    def mix_in(c, columns, heard):
        public = pub[c, :, columns]
        mixed = mix[c, :, columns] + (mess_v[c, :, columns] + heard) * (1.0 / 3.0)
        return step_v[c, :, columns] + MIX_RATE * (mixed - public), public, mixed

    def encode(t):
        c = t % chunks

        @pl.when(t < chunks)
        def _():
            for copy in state_loads(c):
                copy.wait()

        arrived(ACROSS, t)
        gradient = add(part.at[t, OWN_MINE], inbox.at[t, NEAR_M], inbox.at[t, IN_SUM_M], inbox.at[t, IN_ACROSS])
        gout[t] = code(c, slice(0, w), gradient)
        start(GO_AFTER, t)
        start(GO_BEFORE, t)

    def update(t):
        c = t % chunks
        arrived(GOSSIP, t)
        params, public, mixed = mix_in(c, slice(0, w), add(inbox.at[t, IN_BEFORE], inbox.at[t, IN_AFTER]))

        @pl.when(t < (rounds - 1) * chunks)
        def _():
            mix[c] = mixed
            par[c] = params

        @pl.when(t >= (rounds - 1) * chunks)
        def _():
            opar[0, :, cols(c)] = params
            opub[0, :, cols(c)] = public
            omix[0, :, cols(c)] = mixed

    def lands(group, k):
        return (LANDS_X_FIRST if k < 2 else LANDS_Z_FIRST)[group]

    def place_of(k):
        return chunks - 2 + k // 2, slice(k % 2 * wl, k % 2 * wl + wl)

    def last_start(k, src, slot, device, group):
        pltpu.make_async_remote_copy(
            src_ref=src, dst_ref=last_inbox.at[k, pl.ds(slot, src.shape[0])], send_sem=send_sem.at[1],
            recv_sem=last_recv_sem.at[group, k], device_id=device, device_id_type=MESH).start()

    def last_arrived(group, k):
        first, blocks = lands(group, k)
        blocks = last_inbox.at[k, pl.ds(first, blocks)]
        pltpu.make_async_copy(blocks, blocks, last_recv_sem.at[group, k]).wait()

    beyond = ((2, opposite), (1, right), (3, left))

    def last_send_parts(k):
        for d, device in beyond:
            last_start(k, last_part.at[k, pl.ds(2 * d, 2)], 2 * d - 2, device, PARTS)

    def last_over_z(k):
        last_arrived(PARTS, k)
        last_zout[k] = add(*[last_part.at[k, 1]] + [last_inbox.at[k, i] for i in (1, 3, 5)]).astype(jnp.bfloat16)
        last_start(k, last_zout.at[pl.ds(k, 1)], lands(ACROSS, k)[0], across, ACROSS)

    def early_over_z(k):
        last_start(k, last_part.at[k, pl.ds(XSIDE, XSIDE)], 0, across, ACROSS)

    def late_send_parts(k):
        last_arrived(ACROSS, k)
        for d, device in beyond:
            last_sums[k - 2, d - 1] = add(last_part.at[k, d], last_inbox.at[k, d]).astype(jnp.bfloat16)
            last_start(k, last_sums.at[k - 2, pl.ds(d - 1, 1)], lands(PARTS, k)[0] + d - 1, device, PARTS)

    def last_encode(k):
        last_arrived(ACROSS if k < 2 else PARTS, k)
        gradient = add(*[last_part.at[k, 0]] + [last_inbox.at[k, i] for i in ((0, 2, 4, 6) if k < 2 else (0, 4, 5, 6))])
        c, columns = place_of(k)
        last_gout[k] = code(c, columns, gradient)
        first = lands(GOSSIP, k)[0]
        last_start(k, last_gout.at[pl.ds(k, 1)], first, after, GOSSIP)
        last_start(k, last_gout.at[pl.ds(k, 1)], first + 1, before, GOSSIP)

    def last_update(k):
        last_arrived(GOSSIP, k)
        c, columns = place_of(k)
        first = lands(GOSSIP, k)[0]
        params, public, mixed = mix_in(c, columns, add(last_inbox.at[k, first], last_inbox.at[k, first + 1]))
        there = pl.ds(c * w + columns.start, wl)
        opar[0, :, there] = params
        opub[0, :, there] = public
        omix[0, :, there] = mixed

    block = lax.broadcasted_iota(jnp.int32, pool.shape, 0) % LANES // BLOCK
    lane_block = lax.broadcasted_iota(jnp.int32, pool.shape, 1) // BLOCK

    hid_load.wait()
    hid_t[0] = hid[0].T
    multiply(0)
    pl.semaphore_wait(barrier, 6)
    send_parts(0)

    @pl.loop(AHEAD, items + 2)
    def _(t):
        cot_load(t).start()

    @pl.loop(0, chunks)
    def _(c):
        for copy in state_loads(c):
            copy.start()

    for t in range(1, AHEAD):
        multiply(t)
        send_parts(t)
    for r in range(1, rounds):
        hid_t[r] = hid[r].T
    pool[...] = (block == lane_block).astype(jnp.bfloat16)

    multiply_last(1)
    early_over_z(2)
    early_over_z(3)

    @pl.loop(AHEAD, items)
    def _(t):
        multiply(t)

    multiply_last(0)

    def stage(work, item):
        @pl.when((item >= 0) & (item < items))
        def _():
            work(item)

    late = {items - 3: ((last_send_parts, 0),), items - 2: ((last_send_parts, 1),),
            items - 1: ((late_send_parts, 2), (late_send_parts, 3)),
            items: ((last_over_z, 0),), items + 1: ((last_over_z, 1),),
            items + 3: ((last_encode, 0), (last_encode, 2), (last_encode, 3)), items + 4: ((last_encode, 1),),
            items + 5: ((last_update, 0), (last_update, 2), (last_update, 3), (last_update, 1))}

    @pl.loop(0, items + LAGS[-1])
    def _(t):
        stage(pass_on, t)
        stage(send_parts, t + AHEAD)
        stage(over_z, t - LAGS[0])
        stage(update, t - LAGS[2])
        for step, works in late.items():
            @pl.when(t == step)
            def _():
                for work, k in works:
                    work(k)
        stage(encode, t - LAGS[1])

    pltpu.make_async_copy(inbox, inbox, send_sem.at[0]).wait()
    pltpu.make_async_copy(last_inbox, last_inbox, send_sem.at[1]).wait()


def deliver(*refs):
    sem = refs[-1]
    arrays = (len(refs) - 1) // 2
    copies = []
    for i in range(arrays):
        half = refs[i].shape[1] // 2
        for j in range(2):
            piece = (0, pl.ds(j * half, half))
            copies.append(pltpu.make_async_copy(refs[i].at[piece], refs[arrays + i].at[piece], sem.at[i, j]))
    for copy in copies:
        copy.start()
    for copy in copies:
        copy.wait()


def per_device(params, public, mixed, hidden, cotangent):
    _, rows, width = params.shape
    _, rounds, tokens, rows_all = hidden.shape
    items = rounds * CHUNKS - 2
    w = width // CHUNKS
    piece = pltpu.VMEM((items, rows, w), jnp.bfloat16)
    state = pltpu.VMEM((CHUNKS, rows, w), jnp.float32)
    anywhere = pl.BlockSpec(memory_space=pl.ANY)
    in_vmem = pl.BlockSpec(memory_space=pltpu.VMEM)
    results = pl.pallas_call(
        kernel,
        out_shape=(pltpu.VMEM(params.shape, jnp.float32),) * 3,
        in_specs=[anywhere] * 5,
        out_specs=(in_vmem,) * 3,
        scratch_shapes=[
            pltpu.VMEM((rounds, tokens, rows_all), jnp.bfloat16),
            pltpu.VMEM((rounds, rows_all, tokens), jnp.bfloat16),
            pltpu.VMEM((items + 2, tokens, w), jnp.bfloat16),
            state, state, state,
            pltpu.VMEM((items, rows_all // rows, rows, w), jnp.bfloat16),
            pltpu.VMEM((items, INBOX, rows, w), jnp.bfloat16),
            *[piece] * 4,
            state, state,
            pltpu.VMEM((2 * LANES, LANES), jnp.bfloat16),
            pltpu.VMEM((PIECES, rows_all // rows, rows, w // 2), jnp.bfloat16),
            pltpu.VMEM((PIECES, INBOX, rows, w // 2), jnp.bfloat16),
            pltpu.VMEM((2, rows, w // 2), jnp.bfloat16),
            pltpu.VMEM((2, XSIDE - 1, rows, w // 2), jnp.bfloat16),
            pltpu.VMEM((PIECES, rows, w // 2), jnp.bfloat16),
            pltpu.SemaphoreType.DMA((1,)),
            pltpu.SemaphoreType.DMA((items + 2,)),
            pltpu.SemaphoreType.DMA((3, CHUNKS)),
            pltpu.SemaphoreType.DMA((2,)),
            pltpu.SemaphoreType.DMA((len(LANDS), items)),
            pltpu.SemaphoreType.DMA((len(LANDS), PIECES)),
        ],
        compiler_params=pltpu.CompilerParams(
            collective_id=0, has_side_effects=True, vmem_limit_bytes=40 * 1024 * 1024),
        cost_estimate=pl.CostEstimate(flops=340_000_000, bytes_accessed=5_000_000, transcendentals=0),
    )(*[pltpu.with_memory_space_constraint(a, pltpu.HBM) for a in (params, public, mixed, hidden, cotangent)])
    return pl.pallas_call(
        deliver,
        out_shape=(jax.ShapeDtypeStruct(params.shape, jnp.float32),) * 3,
        in_specs=[in_vmem] * 3,
        out_specs=(anywhere,) * 3,
        scratch_shapes=[pltpu.SemaphoreType.DMA((3, 2))],
        compiler_params=pltpu.CompilerParams(vmem_limit_bytes=1024 * 1024),
    )(*[pltpu.with_memory_space_constraint(a, pltpu.VMEM) for a in results])


def solution(mesh):
    state = P("blk", "fsdp", None)
    tokens = P("blk", None, "fsdp", None)
    return jax.shard_map(
        per_device,
        mesh=mesh,
        in_specs=(state, state, state, tokens, tokens),
        out_specs=(state, state, state),
        check_vma=False,
    )
```

```python
import functools

import jax
import jax.numpy as jnp
from jax import lax
from jax.experimental import pallas as pl
from jax.experimental.pallas import tpu as pltpu
from jax.sharding import PartitionSpec as P

MESH = pl.DeviceIdType.MESH
BLOCK = 32
LANES = 128
LEARN_RATE = 0.25
MIX_RATE = 0.4
SCALE_FLOOR = 0.25
CODE_LIMIT = 2.0
CHUNKS = 5
XSIDE = 4
AHEAD = 3
LAGS = (2, 4, 6)

TO_RIGHT, TO_LEFT, SUM_O, SUM_M, OVER, GO_AFTER, GO_BEFORE = range(7)
PARTS, SUMS, ACROSS, GOSSIP = range(4)
LANDS = ((0, 4), (4, 2), (6, 1), (7, 2))
INBOX = 9
NEAR_M, FAR_O, FAR_M, NEAR_O, IN_SUM_O, IN_SUM_M, IN_ACROSS, IN_BEFORE, IN_AFTER = range(INBOX)

PIECES = 4
LANDS_X_FIRST = {PARTS: (0, 6), ACROSS: (6, 1), GOSSIP: (7, 2)}
LANDS_Z_FIRST = {ACROSS: (0, 4), PARTS: (4, 3), GOSSIP: (7, 2)}

OWN_MINE, NEXT_OTHER, LAST_MINE, OWN_OTHER = 0, 1, 2, 3
LEFT_PAIR, RIGHT_PAIR = 4, 6


def tall(wide):
    n = wide.shape[1] // LANES
    return jnp.concatenate([wide[:, i * LANES:(i + 1) * LANES] for i in range(n)], axis=0)


def flat(high, rows):
    n = high.shape[0] // rows
    return jnp.concatenate([high[i * rows:(i + 1) * rows] for i in range(n)], axis=1)


def add(*refs):
    total = refs[0][...].astype(jnp.float32)
    for ref in refs[1:]:
        total = total + ref[...].astype(jnp.float32)
    return total


def kernel(par_hbm, pub_hbm, mix_hbm, hid_hbm, cot_hbm, opar, opub, omix,
           hid, hid_t, cot, par, pub, mix, part, inbox, fwd_o, fwd_m, zout, gout, step_v, mess_v, pool,
           last_part, last_inbox, last_zout, last_sums, last_gout,
           hid_sem, cot_sem, state_sem, send_sem, recv_sem, last_recv_sem):
    rounds, tokens, rows_all = hid.shape
    chunks, rows, w = par.shape
    items = rounds * chunks - 2
    wl = w // 2

    b = lax.axis_index("blk")
    f = lax.axis_index("fsdp")
    nb = lax.axis_size("blk")
    x, zh = f // 2, f % 2
    right = (b, (x + 1) % XSIDE * 2 + zh)
    left = (b, (x + XSIDE - 1) % XSIDE * 2 + zh)
    across = (b, x * 2 + 1 - zh)
    opposite = (b, (x + 2) % XSIDE * 2 + zh)
    after = ((b + 1) % nb, f)
    before = ((b + nb - 1) % nb, f)

    barrier = pltpu.get_barrier_semaphore()
    for device in (right, left, opposite, across, after, before):
        pl.semaphore_signal(barrier, inc=1, device_id=device, device_id_type=MESH)

    def cols(c):
        return pl.ds(pl.multiple_of(c * w, LANES), w)

    def chunk_of(t):
        if isinstance(t, int) and t >= items:
            return 1 - (t - items)
        return t - t // chunks * (chunks - 2)

    hid_load = pltpu.make_async_copy(hid_hbm.at[0], hid, hid_sem.at[0])

    def cot_load(t):
        return pltpu.make_async_copy(cot_hbm.at[0, t // chunks, :, cols(chunk_of(t))], cot.at[t], cot_sem.at[t])

    def state_loads(c):
        return [pltpu.make_async_copy(src.at[0, :, cols(c)], dst.at[c], state_sem.at[i, c])
                for i, (src, dst) in enumerate(((par_hbm, par), (pub_hbm, pub), (mix_hbm, mix)))]

    hid_load.start()
    for t in range(AHEAD):
        cot_load(t).start()

    def land(t, first, blocks=1):
        return inbox.at[t, pl.ds(first, blocks)]

    def start(kind, t):
        src, dst, device, group = {
            TO_RIGHT: lambda: (part.at[t, pl.ds(RIGHT_PAIR, 2)], land(t, NEAR_M, 2), right, PARTS),
            TO_LEFT: lambda: (part.at[t, pl.ds(LEFT_PAIR, 2)], land(t, FAR_M, 2), left, PARTS),
            SUM_O: lambda: (fwd_o.at[pl.ds(t, 1)], land(t, IN_SUM_O), right, SUMS),
            SUM_M: lambda: (fwd_m.at[pl.ds(t, 1)], land(t, IN_SUM_M), left, SUMS),
            OVER: lambda: (zout.at[pl.ds(t, 1)], land(t, IN_ACROSS), across, ACROSS),
            GO_AFTER: lambda: (gout.at[pl.ds(t, 1)], land(t, IN_BEFORE), after, GOSSIP),
            GO_BEFORE: lambda: (gout.at[pl.ds(t, 1)], land(t, IN_AFTER), before, GOSSIP),
        }[kind]()
        pltpu.make_async_remote_copy(
            src_ref=src, dst_ref=dst, send_sem=send_sem.at[0], recv_sem=recv_sem.at[group, t],
            device_id=device, device_id_type=MESH).start()

    def arrived(group, t):
        blocks = land(t, *LANDS[group])
        pltpu.make_async_copy(blocks, blocks, recv_sem.at[group, t]).wait()

    places = [3 * ((j // 2 + XSIDE - x) % XSIDE * 2 + (j + zh) % 2) % 8 for j in range(rows_all // rows)]

    def product(t):
        cot_load(t).wait()
        return jnp.dot(hid_t[t // chunks], cot[t], preferred_element_type=jnp.float32).astype(jnp.bfloat16)

    def multiply(t):
        blocks = product(t)
        for j, place in enumerate(places):
            part[t, place] = blocks[j * rows:(j + 1) * rows]

    def multiply_last(pair):
        blocks = product(items + pair)
        for j, place in enumerate(places):
            which = place * 3 % 8
            if pair == 1:
                which = which % 2 * XSIDE + which // 2
            for i in range(2):
                last_part[2 * pair + i, which] = blocks[j * rows:(j + 1) * rows, i * wl:(i + 1) * wl]

    def send_parts(t):
        start(TO_RIGHT, t)
        start(TO_LEFT, t)

    def pass_on(t):
        arrived(PARTS, t)
        fwd_o[t] = add(inbox.at[t, FAR_O], part.at[t, NEXT_OTHER]).astype(jnp.bfloat16)
        start(SUM_O, t)
        fwd_m[t] = add(inbox.at[t, FAR_M], part.at[t, LAST_MINE]).astype(jnp.bfloat16)
        start(SUM_M, t)

    def over_z(t):
        arrived(SUMS, t)
        zout[t] = add(part.at[t, OWN_OTHER], inbox.at[t, NEAR_O], inbox.at[t, IN_SUM_O]).astype(jnp.bfloat16)
        start(OVER, t)

    def code(c, columns, gradient):
        stepped = par[c, :, columns] - LEARN_RATE * gradient
        public = pub[c, :, columns]
        change = tall(stepped - public)
        square = change * change
        high = square.astype(jnp.bfloat16)
        low = (square - high.astype(jnp.float32)).astype(jnp.bfloat16)
        energy = jnp.dot(jnp.concatenate([high, low], axis=1), pool[...], preferred_element_type=jnp.float32)
        scales = jnp.maximum(jnp.sqrt(energy * (1.0 / BLOCK)), SCALE_FLOOR).astype(jnp.bfloat16)
        wide = scales.astype(jnp.float32)
        coded = jnp.clip(change / wide, -CODE_LIMIT, CODE_LIMIT).astype(jnp.bfloat16)
        message = flat(coded.astype(jnp.float32) * wide, rows)
        pub[c, :, columns] = public + message
        step_v[c, :, columns] = stepped
        mess_v[c, :, columns] = message
        return message.astype(jnp.bfloat16)

    def mix_in(c, columns, heard):
        public = pub[c, :, columns]
        mixed = mix[c, :, columns] + (mess_v[c, :, columns] + heard) * (1.0 / 3.0)
        return step_v[c, :, columns] + MIX_RATE * (mixed - public), public, mixed

    def encode(t):
        c = chunk_of(t)

        @pl.when(t < chunks)
        def _():
            for copy in state_loads(c):
                copy.wait()

        arrived(ACROSS, t)
        gradient = add(part.at[t, OWN_MINE], inbox.at[t, NEAR_M], inbox.at[t, IN_SUM_M], inbox.at[t, IN_ACROSS])
        gout[t] = code(c, slice(0, w), gradient)
        start(GO_AFTER, t)
        start(GO_BEFORE, t)

    def update(t):
        c = chunk_of(t)
        arrived(GOSSIP, t)
        params, public, mixed = mix_in(c, slice(0, w), add(inbox.at[t, IN_BEFORE], inbox.at[t, IN_AFTER]))

        @pl.when(t < (rounds - 1) * chunks)
        def _():
            mix[c] = mixed
            par[c] = params

        @pl.when(t >= (rounds - 1) * chunks)
        def _():
            opar[0, :, cols(c)] = params
            opub[0, :, cols(c)] = public
            omix[0, :, cols(c)] = mixed

    def lands(group, k):
        return (LANDS_X_FIRST if k < 2 else LANDS_Z_FIRST)[group]

    def place_of(k):
        return 1 - k // 2, slice(k % 2 * wl, k % 2 * wl + wl)

    def last_start(k, src, slot, device, group):
        pltpu.make_async_remote_copy(
            src_ref=src, dst_ref=last_inbox.at[k, pl.ds(slot, src.shape[0])], send_sem=send_sem.at[1],
            recv_sem=last_recv_sem.at[group, k], device_id=device, device_id_type=MESH).start()

    def last_arrived(group, k):
        first, blocks = lands(group, k)
        blocks = last_inbox.at[k, pl.ds(first, blocks)]
        pltpu.make_async_copy(blocks, blocks, last_recv_sem.at[group, k]).wait()

    beyond = ((2, opposite), (1, right), (3, left))

    def last_send_parts(k):
        for d, device in beyond:
            last_start(k, last_part.at[k, pl.ds(2 * d, 2)], 2 * d - 2, device, PARTS)

    def last_over_z(k):
        last_arrived(PARTS, k)
        last_zout[k] = add(*[last_part.at[k, 1]] + [last_inbox.at[k, i] for i in (1, 3, 5)]).astype(jnp.bfloat16)
        last_start(k, last_zout.at[pl.ds(k, 1)], lands(ACROSS, k)[0], across, ACROSS)

    def early_over_z(k):
        last_start(k, last_part.at[k, pl.ds(XSIDE, XSIDE)], 0, across, ACROSS)

    def late_send_parts(k):
        last_arrived(ACROSS, k)
        for d, device in beyond:
            last_sums[k - 2, d - 1] = add(last_part.at[k, d], last_inbox.at[k, d]).astype(jnp.bfloat16)
            last_start(k, last_sums.at[k - 2, pl.ds(d - 1, 1)], lands(PARTS, k)[0] + d - 1, device, PARTS)

    def last_encode(k):
        last_arrived(ACROSS if k < 2 else PARTS, k)
        gradient = add(*[last_part.at[k, 0]] + [last_inbox.at[k, i] for i in ((0, 2, 4, 6) if k < 2 else (0, 4, 5, 6))])
        c, columns = place_of(k)
        last_gout[k] = code(c, columns, gradient)
        first = lands(GOSSIP, k)[0]
        last_start(k, last_gout.at[pl.ds(k, 1)], first, after, GOSSIP)
        last_start(k, last_gout.at[pl.ds(k, 1)], first + 1, before, GOSSIP)

    def last_update(k):
        last_arrived(GOSSIP, k)
        c, columns = place_of(k)
        first = lands(GOSSIP, k)[0]
        params, public, mixed = mix_in(c, columns, add(last_inbox.at[k, first], last_inbox.at[k, first + 1]))
        there = pl.ds(c * w + columns.start, wl)
        opar[0, :, there] = params
        opub[0, :, there] = public
        omix[0, :, there] = mixed

    block = lax.broadcasted_iota(jnp.int32, pool.shape, 0) % LANES // BLOCK
    lane_block = lax.broadcasted_iota(jnp.int32, pool.shape, 1) // BLOCK

    hid_load.wait()
    hid_t[0] = hid[0].T
    multiply(0)
    pl.semaphore_wait(barrier, 6)
    send_parts(0)

    for t in (items + 1, items):
        cot_load(t).start()

    @pl.loop(AHEAD, items)
    def _(t):
        cot_load(t).start()

    @pl.loop(0, chunks)
    def _(c):
        for copy in state_loads(c):
            copy.start()

    for t in range(1, AHEAD):
        multiply(t)
        send_parts(t)
    for r in range(1, rounds):
        hid_t[r] = hid[r].T
    pool[...] = (block == lane_block).astype(jnp.bfloat16)

    multiply_last(1)
    early_over_z(2)
    early_over_z(3)

    @pl.loop(AHEAD, items)
    def _(t):
        multiply(t)

    multiply_last(0)

    def stage(work, item):
        @pl.when((item >= 0) & (item < items))
        def _():
            work(item)

    late = {items - 3: ((last_send_parts, 0),), items - 2: ((last_send_parts, 1),),
            items - 1: ((late_send_parts, 2), (late_send_parts, 3)),
            items: ((last_over_z, 0),), items + 1: ((last_over_z, 1), (last_encode, 2), (last_encode, 3)),
            items + 3: ((last_encode, 0), (last_encode, 1)),
            items + 5: ((last_update, 2), (last_update, 3), (last_update, 0), (last_update, 1))}

    @pl.loop(0, items + LAGS[-1])
    def _(t):
        stage(pass_on, t)
        stage(send_parts, t + AHEAD)
        stage(over_z, t - LAGS[0])
        for step, works in late.items():
            @pl.when(t == step)
            def _():
                for work, k in works:
                    work(k)
        stage(encode, t - LAGS[1])
        stage(update, t - LAGS[2])

    pltpu.make_async_copy(inbox, inbox, send_sem.at[0]).wait()
    pltpu.make_async_copy(last_inbox, last_inbox, send_sem.at[1]).wait()


def deliver(*refs):
    sem = refs[-1]
    arrays = (len(refs) - 1) // 2
    copies = []
    for i in range(arrays):
        half = refs[i].shape[1] // 2
        for j in range(2):
            piece = (0, pl.ds(j * half, half))
            copies.append(pltpu.make_async_copy(refs[i].at[piece], refs[arrays + i].at[piece], sem.at[i, j]))
    for copy in copies:
        copy.start()
    for copy in copies:
        copy.wait()


def per_device(params, public, mixed, hidden, cotangent):
    _, rows, width = params.shape
    _, rounds, tokens, rows_all = hidden.shape
    items = rounds * CHUNKS - 2
    w = width // CHUNKS
    piece = pltpu.VMEM((items, rows, w), jnp.bfloat16)
    state = pltpu.VMEM((CHUNKS, rows, w), jnp.float32)
    anywhere = pl.BlockSpec(memory_space=pl.ANY)
    in_vmem = pl.BlockSpec(memory_space=pltpu.VMEM)
    results = pl.pallas_call(
        kernel,
        out_shape=(pltpu.VMEM(params.shape, jnp.float32),) * 3,
        in_specs=[anywhere] * 5,
        out_specs=(in_vmem,) * 3,
        scratch_shapes=[
            pltpu.VMEM((rounds, tokens, rows_all), jnp.bfloat16),
            pltpu.VMEM((rounds, rows_all, tokens), jnp.bfloat16),
            pltpu.VMEM((items + 2, tokens, w), jnp.bfloat16),
            state, state, state,
            pltpu.VMEM((items, rows_all // rows, rows, w), jnp.bfloat16),
            pltpu.VMEM((items, INBOX, rows, w), jnp.bfloat16),
            *[piece] * 4,
            state, state,
            pltpu.VMEM((2 * LANES, LANES), jnp.bfloat16),
            pltpu.VMEM((PIECES, rows_all // rows, rows, w // 2), jnp.bfloat16),
            pltpu.VMEM((PIECES, INBOX, rows, w // 2), jnp.bfloat16),
            pltpu.VMEM((2, rows, w // 2), jnp.bfloat16),
            pltpu.VMEM((2, XSIDE - 1, rows, w // 2), jnp.bfloat16),
            pltpu.VMEM((PIECES, rows, w // 2), jnp.bfloat16),
            pltpu.SemaphoreType.DMA((1,)),
            pltpu.SemaphoreType.DMA((items + 2,)),
            pltpu.SemaphoreType.DMA((3, CHUNKS)),
            pltpu.SemaphoreType.DMA((2,)),
            pltpu.SemaphoreType.DMA((len(LANDS), items)),
            pltpu.SemaphoreType.DMA((len(LANDS), PIECES)),
        ],
        compiler_params=pltpu.CompilerParams(
            collective_id=0, has_side_effects=True, vmem_limit_bytes=40 * 1024 * 1024),
        cost_estimate=pl.CostEstimate(flops=340_000_000, bytes_accessed=5_000_000, transcendentals=0),
    )(*[pltpu.with_memory_space_constraint(a, pltpu.HBM) for a in (params, public, mixed, hidden, cotangent)])
    return pl.pallas_call(
        deliver,
        out_shape=(jax.ShapeDtypeStruct(params.shape, jnp.float32),) * 3,
        in_specs=[in_vmem] * 3,
        out_specs=(anywhere,) * 3,
        scratch_shapes=[pltpu.SemaphoreType.DMA((3, 2))],
        compiler_params=pltpu.CompilerParams(vmem_limit_bytes=1024 * 1024),
    )(*[pltpu.with_memory_space_constraint(a, pltpu.VMEM) for a in results])


def solution(mesh):
    state = P("blk", "fsdp", None)
    tokens = P("blk", None, "fsdp", None)
    return jax.shard_map(
        per_device,
        mesh=mesh,
        in_specs=(state, state, state, tokens, tokens),
        out_specs=(state, state, state),
        check_vma=False,
    )
```

```python
import functools

import jax
import jax.numpy as jnp
from jax import lax
from jax.experimental import pallas as pl
from jax.experimental.pallas import tpu as pltpu
from jax.sharding import PartitionSpec as P

MESH = pl.DeviceIdType.MESH
BLOCK = 32
LANES = 128
LEARN_RATE = 0.25
MIX_RATE = 0.4
SCALE_FLOOR = 0.25
CODE_LIMIT = 2.0
CHUNKS = 4
XSIDE = 4
AHEAD = 3
LAGS = (2, 4, 6)

TO_RIGHT, TO_LEFT, SUM_O, SUM_M, OVER, GO_AFTER, GO_BEFORE = range(7)
PARTS, SUMS, ACROSS, GOSSIP = range(4)
LANDS = ((0, 4), (4, 2), (6, 1), (7, 2))
INBOX = 9
NEAR_M, FAR_O, FAR_M, NEAR_O, IN_SUM_O, IN_SUM_M, IN_ACROSS, IN_BEFORE, IN_AFTER = range(INBOX)

PIECES = 4
LANDS_X_FIRST = {PARTS: (0, 6), ACROSS: (6, 1), GOSSIP: (7, 2)}
LANDS_Z_FIRST = {ACROSS: (0, 4), PARTS: (4, 3), GOSSIP: (7, 2)}

OWN_MINE, NEXT_OTHER, LAST_MINE, OWN_OTHER = 0, 1, 2, 3
LEFT_PAIR, RIGHT_PAIR = 4, 6


def tall(wide):
    n = wide.shape[1] // LANES
    return jnp.concatenate([wide[:, i * LANES:(i + 1) * LANES] for i in range(n)], axis=0)


def flat(high, rows):
    n = high.shape[0] // rows
    return jnp.concatenate([high[i * rows:(i + 1) * rows] for i in range(n)], axis=1)


def add(*refs):
    total = refs[0][...].astype(jnp.float32)
    for ref in refs[1:]:
        total = total + ref[...].astype(jnp.float32)
    return total


def kernel(par_hbm, pub_hbm, mix_hbm, hid_hbm, cot_hbm, opar, opub, omix,
           hid, hid_t, cot, par, pub, mix, part, inbox, fwd_o, fwd_m, zout, gout, step_v, mess_v, pool,
           last_part, last_inbox, last_zout, last_sums, last_gout,
           hid_sem, cot_sem, state_sem, send_sem, recv_sem, last_recv_sem):
    rounds, tokens, rows_all = hid.shape
    chunks, rows, w = par.shape
    items = rounds * chunks - 2
    wl = w // 2

    b = lax.axis_index("blk")
    f = lax.axis_index("fsdp")
    nb = lax.axis_size("blk")
    x, zh = f // 2, f % 2
    right = (b, (x + 1) % XSIDE * 2 + zh)
    left = (b, (x + XSIDE - 1) % XSIDE * 2 + zh)
    across = (b, x * 2 + 1 - zh)
    opposite = (b, (x + 2) % XSIDE * 2 + zh)
    after = ((b + 1) % nb, f)
    before = ((b + nb - 1) % nb, f)

    barrier = pltpu.get_barrier_semaphore()
    for device in (right, left, opposite, across, after, before):
        pl.semaphore_signal(barrier, inc=1, device_id=device, device_id_type=MESH)

    def cols(c):
        return pl.ds(pl.multiple_of(c * w, LANES), w)

    def chunk_of(t):
        if isinstance(t, int) and t >= items:
            return 1 - (t - items)
        return t - t // chunks * (chunks - 2)

    hid_load = pltpu.make_async_copy(hid_hbm.at[0], hid, hid_sem.at[0])

    def cot_load(t):
        return pltpu.make_async_copy(cot_hbm.at[0, t // chunks, :, cols(chunk_of(t))], cot.at[t], cot_sem.at[t])

    def state_loads(c):
        return [pltpu.make_async_copy(src.at[0, :, cols(c)], dst.at[c], state_sem.at[i, c])
                for i, (src, dst) in enumerate(((par_hbm, par), (pub_hbm, pub), (mix_hbm, mix)))]

    hid_load.start()
    for t in range(AHEAD):
        cot_load(t).start()

    def land(t, first, blocks=1):
        return inbox.at[t, pl.ds(first, blocks)]

    def start(kind, t):
        src, dst, device, group = {
            TO_RIGHT: lambda: (part.at[t, pl.ds(RIGHT_PAIR, 2)], land(t, NEAR_M, 2), right, PARTS),
            TO_LEFT: lambda: (part.at[t, pl.ds(LEFT_PAIR, 2)], land(t, FAR_M, 2), left, PARTS),
            SUM_O: lambda: (fwd_o.at[pl.ds(t, 1)], land(t, IN_SUM_O), right, SUMS),
            SUM_M: lambda: (fwd_m.at[pl.ds(t, 1)], land(t, IN_SUM_M), left, SUMS),
            OVER: lambda: (zout.at[pl.ds(t, 1)], land(t, IN_ACROSS), across, ACROSS),
            GO_AFTER: lambda: (gout.at[pl.ds(t, 1)], land(t, IN_BEFORE), after, GOSSIP),
            GO_BEFORE: lambda: (gout.at[pl.ds(t, 1)], land(t, IN_AFTER), before, GOSSIP),
        }[kind]()
        pltpu.make_async_remote_copy(
            src_ref=src, dst_ref=dst, send_sem=send_sem.at[0], recv_sem=recv_sem.at[group, t],
            device_id=device, device_id_type=MESH).start()

    def arrived(group, t):
        blocks = land(t, *LANDS[group])
        pltpu.make_async_copy(blocks, blocks, recv_sem.at[group, t]).wait()

    places = [3 * ((j // 2 + XSIDE - x) % XSIDE * 2 + (j + zh) % 2) % 8 for j in range(rows_all // rows)]

    def product(t):
        cot_load(t).wait()
        return jnp.dot(hid_t[t // chunks], cot[t], preferred_element_type=jnp.float32).astype(jnp.bfloat16)

    def multiply(t):
        blocks = product(t)
        for j, place in enumerate(places):
            part[t, place] = blocks[j * rows:(j + 1) * rows]

    def multiply_last(pair):
        blocks = product(items + pair)
        for j, place in enumerate(places):
            which = place * 3 % 8
            if pair == 1:
                which = which % 2 * XSIDE + which // 2
            for i in range(2):
                last_part[2 * pair + i, which] = blocks[j * rows:(j + 1) * rows, i * wl:(i + 1) * wl]

    def send_parts(t):
        start(TO_RIGHT, t)
        start(TO_LEFT, t)

    def pass_on(t):
        arrived(PARTS, t)
        fwd_o[t] = add(inbox.at[t, FAR_O], part.at[t, NEXT_OTHER]).astype(jnp.bfloat16)
        start(SUM_O, t)
        fwd_m[t] = add(inbox.at[t, FAR_M], part.at[t, LAST_MINE]).astype(jnp.bfloat16)
        start(SUM_M, t)

    def over_z(t):
        arrived(SUMS, t)
        zout[t] = add(part.at[t, OWN_OTHER], inbox.at[t, NEAR_O], inbox.at[t, IN_SUM_O]).astype(jnp.bfloat16)
        start(OVER, t)

    def code(c, columns, gradient):
        stepped = par[c, :, columns] - LEARN_RATE * gradient
        public = pub[c, :, columns]
        change = tall(stepped - public)
        square = change * change
        high = square.astype(jnp.bfloat16)
        low = (square - high.astype(jnp.float32)).astype(jnp.bfloat16)
        energy = jnp.dot(jnp.concatenate([high, low], axis=1), pool[...], preferred_element_type=jnp.float32)
        scales = jnp.maximum(jnp.sqrt(energy * (1.0 / BLOCK)), SCALE_FLOOR).astype(jnp.bfloat16)
        wide = scales.astype(jnp.float32)
        coded = jnp.clip(change / wide, -CODE_LIMIT, CODE_LIMIT).astype(jnp.bfloat16)
        message = flat(coded.astype(jnp.float32) * wide, rows)
        pub[c, :, columns] = public + message
        step_v[c, :, columns] = stepped
        mess_v[c, :, columns] = message
        return message.astype(jnp.bfloat16)

    def mix_in(c, columns, heard):
        public = pub[c, :, columns]
        mixed = mix[c, :, columns] + (mess_v[c, :, columns] + heard) * (1.0 / 3.0)
        return step_v[c, :, columns] + MIX_RATE * (mixed - public), public, mixed

    def encode(t):
        c = chunk_of(t)

        @pl.when(t < chunks)
        def _():
            for copy in state_loads(c):
                copy.wait()

        arrived(ACROSS, t)
        gradient = add(part.at[t, OWN_MINE], inbox.at[t, NEAR_M], inbox.at[t, IN_SUM_M], inbox.at[t, IN_ACROSS])
        gout[t] = code(c, slice(0, w), gradient)
        start(GO_AFTER, t)
        start(GO_BEFORE, t)

    def update(t):
        c = chunk_of(t)
        arrived(GOSSIP, t)
        params, public, mixed = mix_in(c, slice(0, w), add(inbox.at[t, IN_BEFORE], inbox.at[t, IN_AFTER]))

        @pl.when(t < (rounds - 1) * chunks)
        def _():
            mix[c] = mixed
            par[c] = params

        @pl.when(t >= (rounds - 1) * chunks)
        def _():
            opar[0, :, cols(c)] = params
            opub[0, :, cols(c)] = public
            omix[0, :, cols(c)] = mixed

    def lands(group, k):
        return (LANDS_X_FIRST if k < 2 else LANDS_Z_FIRST)[group]

    def place_of(k):
        return 1 - k // 2, slice(k % 2 * wl, k % 2 * wl + wl)

    def last_start(k, src, slot, device, group):
        pltpu.make_async_remote_copy(
            src_ref=src, dst_ref=last_inbox.at[k, pl.ds(slot, src.shape[0])], send_sem=send_sem.at[1],
            recv_sem=last_recv_sem.at[group, k], device_id=device, device_id_type=MESH).start()

    def last_arrived(group, k):
        first, blocks = lands(group, k)
        blocks = last_inbox.at[k, pl.ds(first, blocks)]
        pltpu.make_async_copy(blocks, blocks, last_recv_sem.at[group, k]).wait()

    beyond = ((2, opposite), (1, right), (3, left))

    def last_send_parts(k):
        for d, device in beyond:
            last_start(k, last_part.at[k, pl.ds(2 * d, 2)], 2 * d - 2, device, PARTS)

    def last_over_z(k):
        last_arrived(PARTS, k)
        last_zout[k] = add(*[last_part.at[k, 1]] + [last_inbox.at[k, i] for i in (1, 3, 5)]).astype(jnp.bfloat16)
        last_start(k, last_zout.at[pl.ds(k, 1)], lands(ACROSS, k)[0], across, ACROSS)

    def early_over_z(k):
        last_start(k, last_part.at[k, pl.ds(XSIDE, XSIDE)], 0, across, ACROSS)

    def late_send_parts(k):
        last_arrived(ACROSS, k)
        for d, device in beyond:
            last_sums[k - 2, d - 1] = add(last_part.at[k, d], last_inbox.at[k, d]).astype(jnp.bfloat16)
            last_start(k, last_sums.at[k - 2, pl.ds(d - 1, 1)], lands(PARTS, k)[0] + d - 1, device, PARTS)

    def last_encode(k):
        last_arrived(ACROSS if k < 2 else PARTS, k)
        gradient = add(*[last_part.at[k, 0]] + [last_inbox.at[k, i] for i in ((0, 2, 4, 6) if k < 2 else (0, 4, 5, 6))])
        c, columns = place_of(k)
        last_gout[k] = code(c, columns, gradient)
        first = lands(GOSSIP, k)[0]
        last_start(k, last_gout.at[pl.ds(k, 1)], first, after, GOSSIP)
        last_start(k, last_gout.at[pl.ds(k, 1)], first + 1, before, GOSSIP)

    def last_update(k):
        last_arrived(GOSSIP, k)
        c, columns = place_of(k)
        first = lands(GOSSIP, k)[0]
        params, public, mixed = mix_in(c, columns, add(last_inbox.at[k, first], last_inbox.at[k, first + 1]))
        there = pl.ds(c * w + columns.start, wl)
        opar[0, :, there] = params
        opub[0, :, there] = public
        omix[0, :, there] = mixed

    block = lax.broadcasted_iota(jnp.int32, pool.shape, 0) % LANES // BLOCK
    lane_block = lax.broadcasted_iota(jnp.int32, pool.shape, 1) // BLOCK

    hid_load.wait()
    hid_t[0] = hid[0].T
    multiply(0)
    pl.semaphore_wait(barrier, 6)
    send_parts(0)

    for t in (items + 1, items):
        cot_load(t).start()

    @pl.loop(AHEAD, items)
    def _(t):
        cot_load(t).start()

    @pl.loop(0, chunks)
    def _(c):
        for copy in state_loads(c):
            copy.start()

    for t in range(1, AHEAD):
        multiply(t)
        send_parts(t)
    for r in range(1, rounds):
        hid_t[r] = hid[r].T
    pool[...] = (block == lane_block).astype(jnp.bfloat16)

    multiply_last(1)
    early_over_z(2)
    early_over_z(3)

    @pl.loop(AHEAD, items)
    def _(t):
        multiply(t)

    multiply_last(0)

    def stage(work, item):
        @pl.when((item >= 0) & (item < items))
        def _():
            work(item)

    late = {items - 3: ((last_send_parts, 0),), items - 2: ((last_send_parts, 1),),
            items - 1: ((late_send_parts, 2), (late_send_parts, 3)),
            items: ((last_over_z, 0),), items + 1: ((last_over_z, 1),),
            items + 2: ((last_encode, 2), (last_encode, 3)),
            items + 3: ((last_encode, 0), (last_encode, 1)),
            items + 5: ((last_update, 2), (last_update, 3), (last_update, 0), (last_update, 1))}

    @pl.loop(0, items + LAGS[-1])
    def _(t):
        stage(pass_on, t)
        stage(send_parts, t + AHEAD)
        stage(over_z, t - LAGS[0])
        for step, works in late.items():
            @pl.when(t == step)
            def _():
                for work, k in works:
                    work(k)
        stage(update, t - LAGS[2])
        stage(encode, t - LAGS[1])

    pltpu.make_async_copy(inbox, inbox, send_sem.at[0]).wait()
    pltpu.make_async_copy(last_inbox, last_inbox, send_sem.at[1]).wait()


def deliver(*refs):
    sem = refs[-1]
    arrays = (len(refs) - 1) // 2
    copies = []
    for i in range(arrays):
        half, part = refs[i].shape[1] // 2, refs[i].shape[2] // 2
        for j in range(4):
            piece = (0, pl.ds(j // 2 * half, half), pl.ds(j % 2 * part, part))
            copies.append(pltpu.make_async_copy(refs[i].at[piece], refs[arrays + i].at[piece], sem.at[i, j]))
    for copy in copies:
        copy.start()
    for copy in copies:
        copy.wait()


def per_device(params, public, mixed, hidden, cotangent):
    _, rows, width = params.shape
    _, rounds, tokens, rows_all = hidden.shape
    items = rounds * CHUNKS - 2
    w = width // CHUNKS
    piece = pltpu.VMEM((items, rows, w), jnp.bfloat16)
    state = pltpu.VMEM((CHUNKS, rows, w), jnp.float32)
    anywhere = pl.BlockSpec(memory_space=pl.ANY)
    in_vmem = pl.BlockSpec(memory_space=pltpu.VMEM)
    results = pl.pallas_call(
        kernel,
        out_shape=(pltpu.VMEM(params.shape, jnp.float32),) * 3,
        in_specs=[anywhere] * 5,
        out_specs=(in_vmem,) * 3,
        scratch_shapes=[
            pltpu.VMEM((rounds, tokens, rows_all), jnp.bfloat16),
            pltpu.VMEM((rounds, rows_all, tokens), jnp.bfloat16),
            pltpu.VMEM((items + 2, tokens, w), jnp.bfloat16),
            state, state, state,
            pltpu.VMEM((items, rows_all // rows, rows, w), jnp.bfloat16),
            pltpu.VMEM((items, INBOX, rows, w), jnp.bfloat16),
            *[piece] * 4,
            state, state,
            pltpu.VMEM((2 * LANES, LANES), jnp.bfloat16),
            pltpu.VMEM((PIECES, rows_all // rows, rows, w // 2), jnp.bfloat16),
            pltpu.VMEM((PIECES, INBOX, rows, w // 2), jnp.bfloat16),
            pltpu.VMEM((2, rows, w // 2), jnp.bfloat16),
            pltpu.VMEM((2, XSIDE - 1, rows, w // 2), jnp.bfloat16),
            pltpu.VMEM((PIECES, rows, w // 2), jnp.bfloat16),
            pltpu.SemaphoreType.DMA((1,)),
            pltpu.SemaphoreType.DMA((items + 2,)),
            pltpu.SemaphoreType.DMA((3, CHUNKS)),
            pltpu.SemaphoreType.DMA((2,)),
            pltpu.SemaphoreType.DMA((len(LANDS), items)),
            pltpu.SemaphoreType.DMA((len(LANDS), PIECES)),
        ],
        compiler_params=pltpu.CompilerParams(
            collective_id=0, has_side_effects=True, vmem_limit_bytes=40 * 1024 * 1024),
        cost_estimate=pl.CostEstimate(flops=340_000_000, bytes_accessed=5_000_000, transcendentals=0),
    )(*[pltpu.with_memory_space_constraint(a, pltpu.HBM) for a in (params, public, mixed, hidden, cotangent)])
    return pl.pallas_call(
        deliver,
        out_shape=(jax.ShapeDtypeStruct(params.shape, jnp.float32),) * 3,
        in_specs=[in_vmem] * 3,
        out_specs=(anywhere,) * 3,
        scratch_shapes=[pltpu.SemaphoreType.DMA((3, 4))],
        compiler_params=pltpu.CompilerParams(vmem_limit_bytes=1024 * 1024),
    )(*[pltpu.with_memory_space_constraint(a, pltpu.VMEM) for a in results])


def solution(mesh):
    state = P("blk", "fsdp", None)
    tokens = P("blk", None, "fsdp", None)
    return jax.shard_map(
        per_device,
        mesh=mesh,
        in_specs=(state, state, state, tokens, tokens),
        out_specs=(state, state, state),
        check_vma=False,
    )
```

```python
import functools

import jax
import jax.numpy as jnp
from jax import lax
from jax.experimental import pallas as pl
from jax.experimental.pallas import tpu as pltpu
from jax.sharding import PartitionSpec as P

MESH = pl.DeviceIdType.MESH
BLOCK = 32
LANES = 128
LEARN_RATE = 0.25
MIX_RATE = 0.4
SCALE_FLOOR = 0.25
CODE_LIMIT = 2.0
CHUNKS = 5
XSIDE = 4
AHEAD = 3
LAGS = (2, 5, 7)

TO_RIGHT, TO_LEFT, SUM_O, SUM_M, OVER, GO_AFTER, GO_BEFORE = range(7)
PARTS, SUMS, ACROSS, GOSSIP = range(4)
LANDS = ((0, 4), (4, 2), (6, 1), (7, 2))
INBOX = 9
NEAR_M, FAR_O, FAR_M, NEAR_O, IN_SUM_O, IN_SUM_M, IN_ACROSS, IN_BEFORE, IN_AFTER = range(INBOX)

PIECES = 4
LANDS_X_FIRST = {PARTS: (0, 6), ACROSS: (6, 1), GOSSIP: (7, 2)}
LANDS_Z_FIRST = {ACROSS: (0, 4), PARTS: (4, 3), GOSSIP: (7, 2)}

OWN_MINE, NEXT_OTHER, LAST_MINE, OWN_OTHER = 0, 1, 2, 3
LEFT_PAIR, RIGHT_PAIR = 4, 6


def tall(wide):
    n = wide.shape[1] // LANES
    return jnp.concatenate([wide[:, i * LANES:(i + 1) * LANES] for i in range(n)], axis=0)


def flat(high, rows):
    n = high.shape[0] // rows
    return jnp.concatenate([high[i * rows:(i + 1) * rows] for i in range(n)], axis=1)


def add(*refs):
    total = refs[0][...].astype(jnp.float32)
    for ref in refs[1:]:
        total = total + ref[...].astype(jnp.float32)
    return total


def kernel(par_hbm, pub_hbm, mix_hbm, hid_hbm, cot_hbm, opar, opub, omix,
           hid, hid_t, cot, par, pub, mix, part, inbox, fwd_o, fwd_m, zout, gout, step_v, mess_v, pool,
           last_part, last_inbox, last_zout, last_sums, last_gout,
           hid_sem, cot_sem, state_sem, send_sem, recv_sem, last_recv_sem):
    rounds, tokens, rows_all = hid.shape
    chunks, rows, w = par.shape
    items = rounds * chunks - 2
    wl = w // 2

    b = lax.axis_index("blk")
    f = lax.axis_index("fsdp")
    nb = lax.axis_size("blk")
    x, zh = f // 2, f % 2
    right = (b, (x + 1) % XSIDE * 2 + zh)
    left = (b, (x + XSIDE - 1) % XSIDE * 2 + zh)
    across = (b, x * 2 + 1 - zh)
    opposite = (b, (x + 2) % XSIDE * 2 + zh)
    after = ((b + 1) % nb, f)
    before = ((b + nb - 1) % nb, f)

    def cols(c):
        return pl.ds(pl.multiple_of(c * w, LANES), w)

    def chunk_of(t):
        if isinstance(t, int) and t >= items:
            return 1 - (t - items)
        return t - t // chunks * (chunks - 2)

    hid_load = pltpu.make_async_copy(hid_hbm.at[0], hid, hid_sem.at[0])

    def cot_load(t):
        return pltpu.make_async_copy(cot_hbm.at[0, t // chunks, :, cols(chunk_of(t))], cot.at[t], cot_sem.at[t])

    def state_loads(c):
        return [pltpu.make_async_copy(src.at[0, :, cols(c)], dst.at[c], state_sem.at[i, c])
                for i, (src, dst) in enumerate(((par_hbm, par), (pub_hbm, pub), (mix_hbm, mix)))]

    def first_loads():
        step = tokens // 4
        return [pltpu.make_async_copy(cot_hbm.at[0, 0, pl.ds(i * step, step), pl.ds(0, w)],
                                      cot.at[0, pl.ds(i * step, step)], hid_sem.at[1 + i]) for i in range(4)]

    hid_load.start()
    for copy in first_loads():
        copy.start()

    barrier = pltpu.get_barrier_semaphore()
    for device in (right, left, opposite, across, after, before):
        pl.semaphore_signal(barrier, inc=1, device_id=device, device_id_type=MESH)

    def land(t, first, blocks=1):
        return inbox.at[t, pl.ds(first, blocks)]

    def start(kind, t):
        src, dst, device, group = {
            TO_RIGHT: lambda: (part.at[t, pl.ds(RIGHT_PAIR, 2)], land(t, NEAR_M, 2), right, PARTS),
            TO_LEFT: lambda: (part.at[t, pl.ds(LEFT_PAIR, 2)], land(t, FAR_M, 2), left, PARTS),
            SUM_O: lambda: (fwd_o.at[pl.ds(t, 1)], land(t, IN_SUM_O), right, SUMS),
            SUM_M: lambda: (fwd_m.at[pl.ds(t, 1)], land(t, IN_SUM_M), left, SUMS),
            OVER: lambda: (zout.at[pl.ds(t, 1)], land(t, IN_ACROSS), across, ACROSS),
            GO_AFTER: lambda: (gout.at[pl.ds(t, 1)], land(t, IN_BEFORE), after, GOSSIP),
            GO_BEFORE: lambda: (gout.at[pl.ds(t, 1)], land(t, IN_AFTER), before, GOSSIP),
        }[kind]()
        pltpu.make_async_remote_copy(
            src_ref=src, dst_ref=dst, send_sem=send_sem.at[0], recv_sem=recv_sem.at[group, t],
            device_id=device, device_id_type=MESH).start()

    def arrived(group, t):
        blocks = land(t, *LANDS[group])
        pltpu.make_async_copy(blocks, blocks, recv_sem.at[group, t]).wait()

    places = [3 * ((j // 2 + XSIDE - x) % XSIDE * 2 + (j + zh) % 2) % 8 for j in range(rows_all // rows)]

    def product(t):
        if not isinstance(t, int) or t > 0:
            cot_load(t).wait()
        else:
            for copy in first_loads():
                copy.wait()
        return jnp.dot(hid_t[t // chunks], cot[t], preferred_element_type=jnp.float32).astype(jnp.bfloat16)

    def multiply(t):
        blocks = product(t)
        for j, place in enumerate(places):
            part[t, place] = blocks[j * rows:(j + 1) * rows]

    def multiply_last(pair):
        blocks = product(items + pair)
        for j, place in enumerate(places):
            which = place * 3 % 8
            if pair == 1:
                which = which % 2 * XSIDE + which // 2
            for i in range(2):
                last_part[2 * pair + i, which] = blocks[j * rows:(j + 1) * rows, i * wl:(i + 1) * wl]

    def send_parts(t):
        start(TO_RIGHT, t)
        start(TO_LEFT, t)

    def pass_on(t):
        arrived(PARTS, t)
        fwd_o[t] = add(inbox.at[t, FAR_O], part.at[t, NEXT_OTHER]).astype(jnp.bfloat16)
        start(SUM_O, t)
        fwd_m[t] = add(inbox.at[t, FAR_M], part.at[t, LAST_MINE]).astype(jnp.bfloat16)
        start(SUM_M, t)

    def over_z(t):
        arrived(SUMS, t)
        zout[t] = add(part.at[t, OWN_OTHER], inbox.at[t, NEAR_O], inbox.at[t, IN_SUM_O]).astype(jnp.bfloat16)
        start(OVER, t)

    def code(c, columns, gradient):
        stepped = par[c, :, columns] - LEARN_RATE * gradient
        public = pub[c, :, columns]
        change = tall(stepped - public)
        square = change * change
        high = square.astype(jnp.bfloat16)
        low = (square - high.astype(jnp.float32)).astype(jnp.bfloat16)
        energy = jnp.dot(jnp.concatenate([high, low], axis=1), pool[...], preferred_element_type=jnp.float32)
        scales = jnp.maximum(jnp.sqrt(energy * (1.0 / BLOCK)), SCALE_FLOOR).astype(jnp.bfloat16)
        wide = scales.astype(jnp.float32)
        coded = jnp.clip(change / wide, -CODE_LIMIT, CODE_LIMIT).astype(jnp.bfloat16)
        message = flat(coded.astype(jnp.float32) * wide, rows)
        pub[c, :, columns] = public + message
        step_v[c, :, columns] = stepped
        mess_v[c, :, columns] = message
        return message.astype(jnp.bfloat16)

    def mix_in(c, columns, heard):
        public = pub[c, :, columns]
        mixed = mix[c, :, columns] + (mess_v[c, :, columns] + heard) * (1.0 / 3.0)
        return step_v[c, :, columns] + MIX_RATE * (mixed - public), public, mixed

    def encode(t):
        c = chunk_of(t)

        @pl.when(t < chunks)
        def _():
            for copy in state_loads(c):
                copy.wait()

        arrived(ACROSS, t)
        gradient = add(part.at[t, OWN_MINE], inbox.at[t, NEAR_M], inbox.at[t, IN_SUM_M], inbox.at[t, IN_ACROSS])
        gout[t] = code(c, slice(0, w), gradient)
        start(GO_AFTER, t)
        start(GO_BEFORE, t)

    def update(t):
        c = chunk_of(t)
        arrived(GOSSIP, t)
        params, public, mixed = mix_in(c, slice(0, w), add(inbox.at[t, IN_BEFORE], inbox.at[t, IN_AFTER]))

        @pl.when(t < (rounds - 1) * chunks)
        def _():
            mix[c] = mixed
            par[c] = params

        @pl.when(t >= (rounds - 1) * chunks)
        def _():
            opar[0, :, cols(c)] = params
            opub[0, :, cols(c)] = public
            omix[0, :, cols(c)] = mixed

    def lands(group, k):
        return (LANDS_X_FIRST if k < 2 else LANDS_Z_FIRST)[group]

    def place_of(k):
        return 1 - k // 2, slice(k % 2 * wl, k % 2 * wl + wl)

    def last_start(k, src, slot, device, group):
        pltpu.make_async_remote_copy(
            src_ref=src, dst_ref=last_inbox.at[k, pl.ds(slot, src.shape[0])], send_sem=send_sem.at[1],
            recv_sem=last_recv_sem.at[group, k], device_id=device, device_id_type=MESH).start()

    def last_arrived(group, k):
        first, blocks = lands(group, k)
        blocks = last_inbox.at[k, pl.ds(first, blocks)]
        pltpu.make_async_copy(blocks, blocks, last_recv_sem.at[group, k]).wait()

    beyond = ((2, opposite), (1, right), (3, left))

    def last_send_parts(k):
        for d, device in beyond:
            last_start(k, last_part.at[k, pl.ds(2 * d, 2)], 2 * d - 2, device, PARTS)

    def last_over_z(k):
        last_arrived(PARTS, k)
        last_zout[k] = add(*[last_part.at[k, 1]] + [last_inbox.at[k, i] for i in (1, 3, 5)]).astype(jnp.bfloat16)
        last_start(k, last_zout.at[pl.ds(k, 1)], lands(ACROSS, k)[0], across, ACROSS)

    def early_over_z(k):
        last_start(k, last_part.at[k, pl.ds(XSIDE, XSIDE)], 0, across, ACROSS)

    def late_send_parts(k):
        last_arrived(ACROSS, k)
        for d, device in beyond:
            last_sums[k - 2, d - 1] = add(last_part.at[k, d], last_inbox.at[k, d]).astype(jnp.bfloat16)
            last_start(k, last_sums.at[k - 2, pl.ds(d - 1, 1)], lands(PARTS, k)[0] + d - 1, device, PARTS)

    def last_encode(k):
        last_arrived(ACROSS if k < 2 else PARTS, k)
        gradient = add(*[last_part.at[k, 0]] + [last_inbox.at[k, i] for i in ((0, 2, 4, 6) if k < 2 else (0, 4, 5, 6))])
        c, columns = place_of(k)
        last_gout[k] = code(c, columns, gradient)
        first = lands(GOSSIP, k)[0]
        last_start(k, last_gout.at[pl.ds(k, 1)], first, after, GOSSIP)
        last_start(k, last_gout.at[pl.ds(k, 1)], first + 1, before, GOSSIP)

    def last_update(k):
        last_arrived(GOSSIP, k)
        c, columns = place_of(k)
        first = lands(GOSSIP, k)[0]
        params, public, mixed = mix_in(c, columns, add(last_inbox.at[k, first], last_inbox.at[k, first + 1]))
        there = pl.ds(c * w + columns.start, wl)
        opar[0, :, there] = params
        opub[0, :, there] = public
        omix[0, :, there] = mixed

    block = lax.broadcasted_iota(jnp.int32, pool.shape, 0) % LANES // BLOCK
    lane_block = lax.broadcasted_iota(jnp.int32, pool.shape, 1) // BLOCK

    hid_load.wait()
    hid_t[0] = hid[0].T
    multiply(0)
    pl.semaphore_wait(barrier, 6)
    send_parts(0)

    for t in (*range(1, AHEAD), items + 1, items):
        cot_load(t).start()

    @pl.loop(AHEAD, items)
    def _(t):
        cot_load(t).start()

    @pl.loop(0, chunks)
    def _(c):
        for copy in state_loads(c):
            copy.start()

    for t in range(1, AHEAD):
        multiply(t)
        send_parts(t)
    for r in range(1, rounds):
        hid_t[r] = hid[r].T
    pool[...] = (block == lane_block).astype(jnp.bfloat16)

    multiply_last(1)
    early_over_z(2)
    early_over_z(3)

    @pl.loop(AHEAD, items)
    def _(t):
        multiply(t)

    multiply_last(0)

    def stage(work, item):
        @pl.when((item >= 0) & (item < items))
        def _():
            work(item)

    late = {items - 3: ((last_send_parts, 0),), items - 2: ((last_send_parts, 1),),
            items - 1: ((late_send_parts, 2), (late_send_parts, 3)),
            items: ((last_over_z, 0),), items + 1: ((last_over_z, 1),),
            items + 2: ((last_encode, 2), (last_encode, 3)),
            items + 3: ((last_encode, 0), (last_encode, 1)),
            items + 6: ((last_update, 2), (last_update, 3), (last_update, 0), (last_update, 1))}

    @pl.loop(0, items + LAGS[-1])
    def _(t):
        stage(pass_on, t)
        stage(send_parts, t + AHEAD)
        stage(over_z, t - LAGS[0])
        for step, works in late.items():
            @pl.when(t == step)
            def _():
                for work, k in works:
                    work(k)
        stage(encode, t - LAGS[1])
        stage(update, t - LAGS[2])

    pltpu.make_async_copy(inbox, inbox, send_sem.at[0]).wait()
    pltpu.make_async_copy(last_inbox, last_inbox, send_sem.at[1]).wait()


def deliver(*refs):
    sem = refs[-1]
    arrays = (len(refs) - 1) // 2
    copies = []
    for i in range(arrays):
        half = refs[i].shape[1] // 2
        for j in range(2):
            piece = (0, pl.ds(j * half, half))
            copies.append(pltpu.make_async_copy(refs[i].at[piece], refs[arrays + i].at[piece], sem.at[i, j]))
    for copy in copies:
        copy.start()
    for copy in copies:
        copy.wait()


def per_device(params, public, mixed, hidden, cotangent):
    _, rows, width = params.shape
    _, rounds, tokens, rows_all = hidden.shape
    items = rounds * CHUNKS - 2
    w = width // CHUNKS
    piece = pltpu.VMEM((items, rows, w), jnp.bfloat16)
    state = pltpu.VMEM((CHUNKS, rows, w), jnp.float32)
    anywhere = pl.BlockSpec(memory_space=pl.ANY)
    in_vmem = pl.BlockSpec(memory_space=pltpu.VMEM)
    results = pl.pallas_call(
        kernel,
        out_shape=(pltpu.VMEM(params.shape, jnp.float32),) * 3,
        in_specs=[anywhere] * 5,
        out_specs=(in_vmem,) * 3,
        scratch_shapes=[
            pltpu.VMEM((rounds, tokens, rows_all), jnp.bfloat16),
            pltpu.VMEM((rounds, rows_all, tokens), jnp.bfloat16),
            pltpu.VMEM((items + 2, tokens, w), jnp.bfloat16),
            state, state, state,
            pltpu.VMEM((items, rows_all // rows, rows, w), jnp.bfloat16),
            pltpu.VMEM((items, INBOX, rows, w), jnp.bfloat16),
            *[piece] * 4,
            state, state,
            pltpu.VMEM((2 * LANES, LANES), jnp.bfloat16),
            pltpu.VMEM((PIECES, rows_all // rows, rows, w // 2), jnp.bfloat16),
            pltpu.VMEM((PIECES, INBOX, rows, w // 2), jnp.bfloat16),
            pltpu.VMEM((2, rows, w // 2), jnp.bfloat16),
            pltpu.VMEM((2, XSIDE - 1, rows, w // 2), jnp.bfloat16),
            pltpu.VMEM((PIECES, rows, w // 2), jnp.bfloat16),
            pltpu.SemaphoreType.DMA((5,)),
            pltpu.SemaphoreType.DMA((items + 2,)),
            pltpu.SemaphoreType.DMA((3, CHUNKS)),
            pltpu.SemaphoreType.DMA((2,)),
            pltpu.SemaphoreType.DMA((len(LANDS), items)),
            pltpu.SemaphoreType.DMA((len(LANDS), PIECES)),
        ],
        compiler_params=pltpu.CompilerParams(
            collective_id=0, has_side_effects=True, vmem_limit_bytes=40 * 1024 * 1024),
        cost_estimate=pl.CostEstimate(flops=340_000_000, bytes_accessed=5_000_000, transcendentals=0),
    )(*[pltpu.with_memory_space_constraint(a, pltpu.HBM) for a in (params, public, mixed, hidden, cotangent)])
    return pl.pallas_call(
        deliver,
        out_shape=(jax.ShapeDtypeStruct(params.shape, jnp.float32),) * 3,
        in_specs=[in_vmem] * 3,
        out_specs=(anywhere,) * 3,
        scratch_shapes=[pltpu.SemaphoreType.DMA((3, 2))],
        compiler_params=pltpu.CompilerParams(vmem_limit_bytes=1024 * 1024),
    )(*[pltpu.with_memory_space_constraint(a, pltpu.VMEM) for a in results])


def solution(mesh):
    state = P("blk", "fsdp", None)
    tokens = P("blk", None, "fsdp", None)
    return jax.shard_map(
        per_device,
        mesh=mesh,
        in_specs=(state, state, state, tokens, tokens),
        out_specs=(state, state, state),
        check_vma=False,
    )
```

```python
import functools

import jax
import jax.numpy as jnp
from jax import lax
from jax.experimental import pallas as pl
from jax.experimental.pallas import tpu as pltpu
from jax.sharding import PartitionSpec as P

MESH = pl.DeviceIdType.MESH
BLOCK = 32
LANES = 128
LEARN_RATE = 0.25
MIX_RATE = 0.4
SCALE_FLOOR = 0.25
CODE_LIMIT = 2.0
CHUNKS = 5
XSIDE = 4
AHEAD = 3
EARLY = 5
LAGS = (2, 4, 6)

TO_RIGHT, TO_LEFT, SUM_O, SUM_M, OVER, GO_AFTER, GO_BEFORE = range(7)
PARTS, SUMS, ACROSS, GOSSIP = range(4)
LANDS = ((0, 4), (4, 2), (6, 1), (7, 2))
INBOX = 9
NEAR_M, FAR_O, FAR_M, NEAR_O, IN_SUM_O, IN_SUM_M, IN_ACROSS, IN_BEFORE, IN_AFTER = range(INBOX)

PIECES = 4
LANDS_X_FIRST = {PARTS: (0, 6), ACROSS: (6, 1), GOSSIP: (7, 2)}
LANDS_Z_FIRST = {ACROSS: (0, 4), PARTS: (4, 3), GOSSIP: (7, 2)}

OWN_MINE, NEXT_OTHER, LAST_MINE, OWN_OTHER = 0, 1, 2, 3
LEFT_PAIR, RIGHT_PAIR = 4, 6


def tall(wide):
    n = wide.shape[1] // LANES
    return jnp.concatenate([wide[:, i * LANES:(i + 1) * LANES] for i in range(n)], axis=0)


def flat(high, rows):
    n = high.shape[0] // rows
    return jnp.concatenate([high[i * rows:(i + 1) * rows] for i in range(n)], axis=1)


def add(*refs):
    total = refs[0][...].astype(jnp.float32)
    for ref in refs[1:]:
        total = total + ref[...].astype(jnp.float32)
    return total


def kernel(par_hbm, pub_hbm, mix_hbm, hid_hbm, cot_hbm, opar, opub, omix,
           hid, hid_t, cot, par, pub, mix, part, inbox, fwd_o, fwd_m, zout, gout, step_v, mess_v, pool,
           last_part, last_inbox, last_zout, last_sums, last_gout,
           hid_sem, cot_sem, state_sem, send_sem, recv_sem, last_recv_sem):
    rounds, tokens, rows_all = hid.shape
    chunks, rows, w = par.shape
    items = rounds * chunks - 2
    wl = w // 2

    b = lax.axis_index("blk")
    f = lax.axis_index("fsdp")
    nb = lax.axis_size("blk")
    x, zh = f // 2, f % 2
    right = (b, (x + 1) % XSIDE * 2 + zh)
    left = (b, (x + XSIDE - 1) % XSIDE * 2 + zh)
    across = (b, x * 2 + 1 - zh)
    opposite = (b, (x + 2) % XSIDE * 2 + zh)
    after = ((b + 1) % nb, f)
    before = ((b + nb - 1) % nb, f)

    def cols(c):
        return pl.ds(pl.multiple_of(c * w, LANES), w)

    def chunk_of(t):
        if isinstance(t, int) and t >= items:
            return 1 - (t - items)
        return t - t // chunks * (chunks - 2)

    hid_load = pltpu.make_async_copy(hid_hbm.at[0], hid, hid_sem.at[0])

    def cot_load(t):
        return pltpu.make_async_copy(cot_hbm.at[0, t // chunks, :, cols(chunk_of(t))], cot.at[t], cot_sem.at[t])

    def state_loads(c):
        return [pltpu.make_async_copy(src.at[0, :, cols(c)], dst.at[c], state_sem.at[i, c])
                for i, (src, dst) in enumerate(((par_hbm, par), (pub_hbm, pub), (mix_hbm, mix)))]

    def first_loads():
        step = tokens // 4
        return [pltpu.make_async_copy(cot_hbm.at[0, 0, pl.ds(i * step, step), pl.ds(0, w)],
                                      cot.at[0, pl.ds(i * step, step)], hid_sem.at[1 + i]) for i in range(4)]

    hid_load.start()
    for copy in first_loads():
        copy.start()

    barrier = pltpu.get_barrier_semaphore()
    for device in (right, left, opposite, across, after, before):
        pl.semaphore_signal(barrier, inc=1, device_id=device, device_id_type=MESH)

    def land(t, first, blocks=1):
        return inbox.at[t, pl.ds(first, blocks)]

    def start(kind, t):
        src, dst, device, group = {
            TO_RIGHT: lambda: (part.at[t, pl.ds(RIGHT_PAIR, 2)], land(t, NEAR_M, 2), right, PARTS),
            TO_LEFT: lambda: (part.at[t, pl.ds(LEFT_PAIR, 2)], land(t, FAR_M, 2), left, PARTS),
            SUM_O: lambda: (fwd_o.at[pl.ds(t, 1)], land(t, IN_SUM_O), right, SUMS),
            SUM_M: lambda: (fwd_m.at[pl.ds(t, 1)], land(t, IN_SUM_M), left, SUMS),
            OVER: lambda: (zout.at[pl.ds(t, 1)], land(t, IN_ACROSS), across, ACROSS),
            GO_AFTER: lambda: (gout.at[pl.ds(t, 1)], land(t, IN_BEFORE), after, GOSSIP),
            GO_BEFORE: lambda: (gout.at[pl.ds(t, 1)], land(t, IN_AFTER), before, GOSSIP),
        }[kind]()
        pltpu.make_async_remote_copy(
            src_ref=src, dst_ref=dst, send_sem=send_sem.at[0], recv_sem=recv_sem.at[group, t],
            device_id=device, device_id_type=MESH).start()

    def arrived(group, t):
        blocks = land(t, *LANDS[group])
        pltpu.make_async_copy(blocks, blocks, recv_sem.at[group, t]).wait()

    places = [3 * ((j // 2 + XSIDE - x) % XSIDE * 2 + (j + zh) % 2) % 8 for j in range(rows_all // rows)]

    def product(t):
        if not isinstance(t, int) or t > 0:
            cot_load(t).wait()
        else:
            for copy in first_loads():
                copy.wait()
        return jnp.dot(hid_t[t // chunks], cot[t], preferred_element_type=jnp.float32).astype(jnp.bfloat16)

    def multiply(t):
        blocks = product(t)
        for j, place in enumerate(places):
            part[t, place] = blocks[j * rows:(j + 1) * rows]

    def multiply_last(pair):
        blocks = product(items + pair)
        for j, place in enumerate(places):
            which = place * 3 % 8
            if pair == 1:
                which = which % 2 * XSIDE + which // 2
            for i in range(2):
                last_part[2 * pair + i, which] = blocks[j * rows:(j + 1) * rows, i * wl:(i + 1) * wl]

    def send_parts(t):
        start(TO_RIGHT, t)
        start(TO_LEFT, t)

    def pass_on(t):
        arrived(PARTS, t)
        fwd_o[t] = add(inbox.at[t, FAR_O], part.at[t, NEXT_OTHER]).astype(jnp.bfloat16)
        start(SUM_O, t)
        fwd_m[t] = add(inbox.at[t, FAR_M], part.at[t, LAST_MINE]).astype(jnp.bfloat16)
        start(SUM_M, t)

    def over_z(t):
        arrived(SUMS, t)
        zout[t] = add(part.at[t, OWN_OTHER], inbox.at[t, NEAR_O], inbox.at[t, IN_SUM_O]).astype(jnp.bfloat16)
        start(OVER, t)

    def code(c, columns, gradient):
        stepped = par[c, :, columns] - LEARN_RATE * gradient
        public = pub[c, :, columns]
        change = tall(stepped - public)
        square = change * change
        high = square.astype(jnp.bfloat16)
        low = (square - high.astype(jnp.float32)).astype(jnp.bfloat16)
        energy = jnp.dot(jnp.concatenate([high, low], axis=1), pool[...], preferred_element_type=jnp.float32)
        scales = jnp.maximum(jnp.sqrt(energy * (1.0 / BLOCK)), SCALE_FLOOR).astype(jnp.bfloat16)
        wide = scales.astype(jnp.float32)
        coded = jnp.clip(change / wide, -CODE_LIMIT, CODE_LIMIT).astype(jnp.bfloat16)
        message = flat(coded.astype(jnp.float32) * wide, rows)
        pub[c, :, columns] = public + message
        step_v[c, :, columns] = stepped
        mess_v[c, :, columns] = message
        return message.astype(jnp.bfloat16)

    def mix_in(c, columns, heard):
        public = pub[c, :, columns]
        mixed = mix[c, :, columns] + (mess_v[c, :, columns] + heard) * (1.0 / 3.0)
        return step_v[c, :, columns] + MIX_RATE * (mixed - public), public, mixed

    def encode(t):
        c = chunk_of(t)

        @pl.when(t < chunks)
        def _():
            for copy in state_loads(c):
                copy.wait()

        arrived(ACROSS, t)
        gradient = add(part.at[t, OWN_MINE], inbox.at[t, NEAR_M], inbox.at[t, IN_SUM_M], inbox.at[t, IN_ACROSS])
        gout[t] = code(c, slice(0, w), gradient)
        start(GO_AFTER, t)
        start(GO_BEFORE, t)

    def update(t):
        c = chunk_of(t)
        arrived(GOSSIP, t)
        params, public, mixed = mix_in(c, slice(0, w), add(inbox.at[t, IN_BEFORE], inbox.at[t, IN_AFTER]))

        @pl.when(t < (rounds - 1) * chunks)
        def _():
            mix[c] = mixed
            par[c] = params

        @pl.when(t >= (rounds - 1) * chunks)
        def _():
            opar[0, :, cols(c)] = params
            opub[0, :, cols(c)] = public
            omix[0, :, cols(c)] = mixed

    def lands(group, k):
        return (LANDS_X_FIRST if k < 2 else LANDS_Z_FIRST)[group]

    def place_of(k):
        return 1 - k // 2, slice(k % 2 * wl, k % 2 * wl + wl)

    def last_start(k, src, slot, device, group):
        pltpu.make_async_remote_copy(
            src_ref=src, dst_ref=last_inbox.at[k, pl.ds(slot, src.shape[0])], send_sem=send_sem.at[1],
            recv_sem=last_recv_sem.at[group, k], device_id=device, device_id_type=MESH).start()

    def last_arrived(group, k):
        first, blocks = lands(group, k)
        blocks = last_inbox.at[k, pl.ds(first, blocks)]
        pltpu.make_async_copy(blocks, blocks, last_recv_sem.at[group, k]).wait()

    beyond = ((2, opposite), (1, right), (3, left))

    def last_send_parts(k):
        for d, device in beyond:
            last_start(k, last_part.at[k, pl.ds(2 * d, 2)], 2 * d - 2, device, PARTS)

    def last_over_z(k):
        last_arrived(PARTS, k)
        last_zout[k] = add(*[last_part.at[k, 1]] + [last_inbox.at[k, i] for i in (1, 3, 5)]).astype(jnp.bfloat16)
        last_start(k, last_zout.at[pl.ds(k, 1)], lands(ACROSS, k)[0], across, ACROSS)

    def early_over_z(k):
        last_start(k, last_part.at[k, pl.ds(XSIDE, XSIDE)], 0, across, ACROSS)

    def late_send_parts(k):
        last_arrived(ACROSS, k)
        for d, device in beyond:
            last_sums[k - 2, d - 1] = add(last_part.at[k, d], last_inbox.at[k, d]).astype(jnp.bfloat16)
            last_start(k, last_sums.at[k - 2, pl.ds(d - 1, 1)], lands(PARTS, k)[0] + d - 1, device, PARTS)

    def last_encode(k):
        last_arrived(ACROSS if k < 2 else PARTS, k)
        gradient = add(*[last_part.at[k, 0]] + [last_inbox.at[k, i] for i in ((0, 2, 4, 6) if k < 2 else (0, 4, 5, 6))])
        c, columns = place_of(k)
        last_gout[k] = code(c, columns, gradient)
        first = lands(GOSSIP, k)[0]
        last_start(k, last_gout.at[pl.ds(k, 1)], first, after, GOSSIP)
        last_start(k, last_gout.at[pl.ds(k, 1)], first + 1, before, GOSSIP)

    def last_update(k):
        last_arrived(GOSSIP, k)
        c, columns = place_of(k)
        first = lands(GOSSIP, k)[0]
        params, public, mixed = mix_in(c, columns, add(last_inbox.at[k, first], last_inbox.at[k, first + 1]))
        there = pl.ds(c * w + columns.start, wl)
        opar[0, :, there] = params
        opub[0, :, there] = public
        omix[0, :, there] = mixed

    block = lax.broadcasted_iota(jnp.int32, pool.shape, 0) % LANES // BLOCK
    lane_block = lax.broadcasted_iota(jnp.int32, pool.shape, 1) // BLOCK

    hid_load.wait()
    hid_t[0] = hid[0].T
    multiply(0)
    pl.semaphore_wait(barrier, 6)
    send_parts(0)

    for t in (*range(1, AHEAD), items + 1, items):
        cot_load(t).start()

    @pl.loop(AHEAD, items)
    def _(t):
        cot_load(t).start()

    @pl.loop(0, chunks)
    def _(c):
        for copy in state_loads(c):
            copy.start()

    for t in range(1, AHEAD):
        multiply(t)
        send_parts(t)
    for r in range(1, rounds):
        hid_t[r] = hid[r].T
    pool[...] = (block == lane_block).astype(jnp.bfloat16)

    multiply_last(1)
    early_over_z(2)
    early_over_z(3)

    for t in range(AHEAD, EARLY):
        multiply(t)

    def stage(work, item):
        @pl.when((item >= 0) & (item < items))
        def _():
            work(item)

    late = {2: ((multiply_last, 0),), items - 3: ((last_send_parts, 0),), items - 2: ((last_send_parts, 1),),
            items - 1: ((late_send_parts, 2), (late_send_parts, 3)),
            items: ((last_over_z, 0),), items + 1: ((last_over_z, 1), (last_encode, 2), (last_encode, 3)),
            items + 3: ((last_encode, 0), (last_encode, 1)),
            items + 5: ((last_update, 2), (last_update, 3), (last_update, 0), (last_update, 1))}

    @pl.loop(0, items + LAGS[-1])
    def _(t):
        stage(pass_on, t)
        stage(send_parts, t + AHEAD)
        stage(over_z, t - LAGS[0])
        for step, works in late.items():
            @pl.when(t == step)
            def _():
                for work, k in works:
                    work(k)
        stage(encode, t - LAGS[1])
        stage(update, t - LAGS[2])
        stage(multiply, t + EARLY)

    pltpu.make_async_copy(inbox, inbox, send_sem.at[0]).wait()
    pltpu.make_async_copy(last_inbox, last_inbox, send_sem.at[1]).wait()


def deliver(*refs):
    sem = refs[-1]
    arrays = (len(refs) - 1) // 2
    copies = []
    for i in range(arrays):
        half = refs[i].shape[1] // 2
        for j in range(2):
            piece = (0, pl.ds(j * half, half))
            copies.append(pltpu.make_async_copy(refs[i].at[piece], refs[arrays + i].at[piece], sem.at[i, j]))
    for copy in copies:
        copy.start()
    for copy in copies:
        copy.wait()


def per_device(params, public, mixed, hidden, cotangent):
    _, rows, width = params.shape
    _, rounds, tokens, rows_all = hidden.shape
    items = rounds * CHUNKS - 2
    w = width // CHUNKS
    piece = pltpu.VMEM((items, rows, w), jnp.bfloat16)
    state = pltpu.VMEM((CHUNKS, rows, w), jnp.float32)
    anywhere = pl.BlockSpec(memory_space=pl.ANY)
    in_vmem = pl.BlockSpec(memory_space=pltpu.VMEM)
    results = pl.pallas_call(
        kernel,
        out_shape=(pltpu.VMEM(params.shape, jnp.float32),) * 3,
        in_specs=[anywhere] * 5,
        out_specs=(in_vmem,) * 3,
        scratch_shapes=[
            pltpu.VMEM((rounds, tokens, rows_all), jnp.bfloat16),
            pltpu.VMEM((rounds, rows_all, tokens), jnp.bfloat16),
            pltpu.VMEM((items + 2, tokens, w), jnp.bfloat16),
            state, state, state,
            pltpu.VMEM((items, rows_all // rows, rows, w), jnp.bfloat16),
            pltpu.VMEM((items, INBOX, rows, w), jnp.bfloat16),
            *[piece] * 4,
            state, state,
            pltpu.VMEM((2 * LANES, LANES), jnp.bfloat16),
            pltpu.VMEM((PIECES, rows_all // rows, rows, w // 2), jnp.bfloat16),
            pltpu.VMEM((PIECES, INBOX, rows, w // 2), jnp.bfloat16),
            pltpu.VMEM((2, rows, w // 2), jnp.bfloat16),
            pltpu.VMEM((2, XSIDE - 1, rows, w // 2), jnp.bfloat16),
            pltpu.VMEM((PIECES, rows, w // 2), jnp.bfloat16),
            pltpu.SemaphoreType.DMA((5,)),
            pltpu.SemaphoreType.DMA((items + 2,)),
            pltpu.SemaphoreType.DMA((3, CHUNKS)),
            pltpu.SemaphoreType.DMA((2,)),
            pltpu.SemaphoreType.DMA((len(LANDS), items)),
            pltpu.SemaphoreType.DMA((len(LANDS), PIECES)),
        ],
        compiler_params=pltpu.CompilerParams(
            collective_id=0, has_side_effects=True, vmem_limit_bytes=40 * 1024 * 1024),
        cost_estimate=pl.CostEstimate(flops=340_000_000, bytes_accessed=5_000_000, transcendentals=0),
    )(*[pltpu.with_memory_space_constraint(a, pltpu.HBM) for a in (params, public, mixed, hidden, cotangent)])
    return pl.pallas_call(
        deliver,
        out_shape=(jax.ShapeDtypeStruct(params.shape, jnp.float32),) * 3,
        in_specs=[in_vmem] * 3,
        out_specs=(anywhere,) * 3,
        scratch_shapes=[pltpu.SemaphoreType.DMA((3, 2))],
        compiler_params=pltpu.CompilerParams(vmem_limit_bytes=1024 * 1024),
    )(*[pltpu.with_memory_space_constraint(a, pltpu.VMEM) for a in results])


def solution(mesh):
    state = P("blk", "fsdp", None)
    tokens = P("blk", None, "fsdp", None)
    return jax.shard_map(
        per_device,
        mesh=mesh,
        in_specs=(state, state, state, tokens, tokens),
        out_specs=(state, state, state),
        check_vma=False,
    )
```

```python
import functools

import jax
import jax.numpy as jnp
from jax import lax
from jax.experimental import pallas as pl
from jax.experimental.pallas import tpu as pltpu
from jax.sharding import PartitionSpec as P

MESH = pl.DeviceIdType.MESH
BLOCK = 32
LANES = 128
LEARN_RATE = 0.25
MIX_RATE = 0.4
SCALE_FLOOR = 0.25
CODE_LIMIT = 2.0
CHUNKS = 5
XSIDE = 4
AHEAD = 3
EARLY = 5
LAGS = (2, 4, 6)

TO_RIGHT, TO_LEFT, SUM_O, SUM_M, OVER, GO_FAR, GO_NEAR = range(7)
PARTS, SUMS, ACROSS, GOSSIP = range(4)
LANDS = ((0, 4), (4, 2), (6, 1), (7, 2))
INBOX = 9
NEAR_M, FAR_O, FAR_M, NEAR_O, IN_SUM_O, IN_SUM_M, IN_ACROSS, IN_FAR, IN_NEAR = range(INBOX)

PIECES = 4
LANDS_X_FIRST = {PARTS: (0, 6), ACROSS: (6, 1), GOSSIP: (7, 2)}
LANDS_Z_FIRST = {ACROSS: (0, 4), PARTS: (4, 3), GOSSIP: (7, 2)}

OWN_MINE, NEXT_OTHER, LAST_MINE, OWN_OTHER = 0, 1, 2, 3
LEFT_PAIR, RIGHT_PAIR = 4, 6


def tall(wide):
    n = wide.shape[1] // LANES
    return jnp.concatenate([wide[:, i * LANES:(i + 1) * LANES] for i in range(n)], axis=0)


def flat(high, rows):
    n = high.shape[0] // rows
    return jnp.concatenate([high[i * rows:(i + 1) * rows] for i in range(n)], axis=1)


def add(*refs):
    total = refs[0][...].astype(jnp.float32)
    for ref in refs[1:]:
        total = total + ref[...].astype(jnp.float32)
    return total


def kernel(par_hbm, pub_hbm, mix_hbm, hid_hbm, cot_hbm, opar, opub, omix,
           hid, hid_t, cot, par, pub, mix, part, inbox, fwd_o, fwd_m, zout, gout, step_v, mess_v, pool,
           last_part, last_inbox, last_zout, last_sums, last_gout,
           hid_sem, cot_sem, state_sem, send_sem, recv_sem, last_recv_sem):
    rounds, tokens, rows_all = hid.shape
    chunks, rows, w = par.shape
    items = rounds * chunks - 2
    wl = w // 2

    b = lax.axis_index("blk")
    f = lax.axis_index("fsdp")
    nb = lax.axis_size("blk")
    x, zh = f // 2, f % 2
    right = (b, (x + 1) % XSIDE * 2 + zh)
    left = (b, (x + XSIDE - 1) % XSIDE * 2 + zh)
    across = (b, x * 2 + 1 - zh)
    opposite = (b, (x + 2) % XSIDE * 2 + zh)
    core = b % 2
    far = ((b + nb - 1 + 2 * core) % nb, f)
    near = (b + 1 - 2 * core, f)

    def cols(c):
        return pl.ds(pl.multiple_of(c * w, LANES), w)

    def chunk_of(t):
        if isinstance(t, int) and t >= items:
            return 1 - (t - items)
        return t - t // chunks * (chunks - 2)

    hid_load = pltpu.make_async_copy(hid_hbm.at[0], hid, hid_sem.at[0])

    def cot_load(t):
        return pltpu.make_async_copy(cot_hbm.at[0, t // chunks, :, cols(chunk_of(t))], cot.at[t], cot_sem.at[t])

    def state_loads(c):
        return [pltpu.make_async_copy(src.at[0, :, cols(c)], dst.at[c], state_sem.at[i, c])
                for i, (src, dst) in enumerate(((par_hbm, par), (pub_hbm, pub), (mix_hbm, mix)))]

    def first_loads():
        step = tokens // 4
        return [pltpu.make_async_copy(cot_hbm.at[0, 0, pl.ds(i * step, step), pl.ds(0, w)],
                                      cot.at[0, pl.ds(i * step, step)], hid_sem.at[1 + i]) for i in range(4)]

    hid_load.start()
    for copy in first_loads():
        copy.start()

    barrier = pltpu.get_barrier_semaphore()
    for device in (right, left, opposite, across, far, near):
        pl.semaphore_signal(barrier, inc=1, device_id=device, device_id_type=MESH)

    def land(t, first, blocks=1):
        return inbox.at[t, pl.ds(first, blocks)]

    def start(kind, t):
        src, dst, device, group = {
            TO_RIGHT: lambda: (part.at[t, pl.ds(RIGHT_PAIR, 2)], land(t, NEAR_M, 2), right, PARTS),
            TO_LEFT: lambda: (part.at[t, pl.ds(LEFT_PAIR, 2)], land(t, FAR_M, 2), left, PARTS),
            SUM_O: lambda: (fwd_o.at[pl.ds(t, 1)], land(t, IN_SUM_O), right, SUMS),
            SUM_M: lambda: (fwd_m.at[pl.ds(t, 1)], land(t, IN_SUM_M), left, SUMS),
            OVER: lambda: (zout.at[pl.ds(t, 1)], land(t, IN_ACROSS), across, ACROSS),
            GO_FAR: lambda: (gout.at[pl.ds(t, 1)], land(t, IN_FAR), far, GOSSIP),
            GO_NEAR: lambda: (gout.at[pl.ds(t, 1)], land(t, IN_NEAR), near, GOSSIP),
        }[kind]()
        pltpu.make_async_remote_copy(
            src_ref=src, dst_ref=dst, send_sem=send_sem.at[0], recv_sem=recv_sem.at[group, t],
            device_id=device, device_id_type=MESH).start()

    def arrived(group, t):
        blocks = land(t, *LANDS[group])
        pltpu.make_async_copy(blocks, blocks, recv_sem.at[group, t]).wait()

    places = [3 * ((j // 2 + XSIDE - x) % XSIDE * 2 + (j + zh) % 2) % 8 for j in range(rows_all // rows)]

    def product(t):
        if not isinstance(t, int) or t > 0:
            cot_load(t).wait()
        else:
            for copy in first_loads():
                copy.wait()
        return jnp.dot(hid_t[t // chunks], cot[t], preferred_element_type=jnp.float32).astype(jnp.bfloat16)

    def multiply(t):
        blocks = product(t)
        for j, place in enumerate(places):
            part[t, place] = blocks[j * rows:(j + 1) * rows]

    def multiply_last(pair):
        blocks = product(items + pair)
        for j, place in enumerate(places):
            which = place * 3 % 8
            if pair == 1:
                which = which % 2 * XSIDE + which // 2
            for i in range(2):
                last_part[2 * pair + i, which] = blocks[j * rows:(j + 1) * rows, i * wl:(i + 1) * wl]

    def send_parts(t):
        start(TO_RIGHT, t)
        start(TO_LEFT, t)

    def pass_on(t):
        arrived(PARTS, t)
        fwd_o[t] = add(inbox.at[t, FAR_O], part.at[t, NEXT_OTHER]).astype(jnp.bfloat16)
        start(SUM_O, t)
        fwd_m[t] = add(inbox.at[t, FAR_M], part.at[t, LAST_MINE]).astype(jnp.bfloat16)
        start(SUM_M, t)

    def over_z(t):
        arrived(SUMS, t)
        zout[t] = add(part.at[t, OWN_OTHER], inbox.at[t, NEAR_O], inbox.at[t, IN_SUM_O]).astype(jnp.bfloat16)
        start(OVER, t)

    def code(c, columns, gradient):
        stepped = par[c, :, columns] - LEARN_RATE * gradient
        public = pub[c, :, columns]
        change = tall(stepped - public)
        square = change * change
        high = square.astype(jnp.bfloat16)
        low = (square - high.astype(jnp.float32)).astype(jnp.bfloat16)
        energy = jnp.dot(jnp.concatenate([high, low], axis=1), pool[...], preferred_element_type=jnp.float32)
        scales = jnp.maximum(jnp.sqrt(energy * (1.0 / BLOCK)), SCALE_FLOOR).astype(jnp.bfloat16)
        wide = scales.astype(jnp.float32)
        coded = jnp.clip(change / wide, -CODE_LIMIT, CODE_LIMIT).astype(jnp.bfloat16)
        message = flat(coded.astype(jnp.float32) * wide, rows)
        pub[c, :, columns] = public + message
        step_v[c, :, columns] = stepped
        mess_v[c, :, columns] = message
        return message.astype(jnp.bfloat16)

    def mix_in(c, columns, heard):
        public = pub[c, :, columns]
        mixed = mix[c, :, columns] + (mess_v[c, :, columns] + heard) * (1.0 / 3.0)
        return step_v[c, :, columns] + MIX_RATE * (mixed - public), public, mixed

    def encode(t):
        c = chunk_of(t)

        @pl.when(t < chunks)
        def _():
            for copy in state_loads(c):
                copy.wait()

        arrived(ACROSS, t)
        gradient = add(part.at[t, OWN_MINE], inbox.at[t, NEAR_M], inbox.at[t, IN_SUM_M], inbox.at[t, IN_ACROSS])
        gout[t] = code(c, slice(0, w), gradient)
        start(GO_FAR, t)
        start(GO_NEAR, t)

    def update(t):
        c = chunk_of(t)
        arrived(GOSSIP, t)
        params, public, mixed = mix_in(c, slice(0, w), add(inbox.at[t, IN_FAR], inbox.at[t, IN_NEAR]))

        @pl.when(t < (rounds - 1) * chunks)
        def _():
            mix[c] = mixed
            par[c] = params

        @pl.when(t >= (rounds - 1) * chunks)
        def _():
            opar[0, :, cols(c)] = params
            opub[0, :, cols(c)] = public
            omix[0, :, cols(c)] = mixed

    def lands(group, k):
        return (LANDS_X_FIRST if k < 2 else LANDS_Z_FIRST)[group]

    def place_of(k):
        return 1 - k // 2, slice(k % 2 * wl, k % 2 * wl + wl)

    def last_start(k, src, slot, device, group):
        pltpu.make_async_remote_copy(
            src_ref=src, dst_ref=last_inbox.at[k, pl.ds(slot, src.shape[0])], send_sem=send_sem.at[1],
            recv_sem=last_recv_sem.at[group, k], device_id=device, device_id_type=MESH).start()

    def last_arrived(group, k):
        first, blocks = lands(group, k)
        blocks = last_inbox.at[k, pl.ds(first, blocks)]
        pltpu.make_async_copy(blocks, blocks, last_recv_sem.at[group, k]).wait()

    beyond = ((2, opposite), (1, right), (3, left))

    def last_send_parts(k):
        for d, device in beyond:
            last_start(k, last_part.at[k, pl.ds(2 * d, 2)], 2 * d - 2, device, PARTS)

    def last_over_z(k):
        last_arrived(PARTS, k)
        last_zout[k] = add(*[last_part.at[k, 1]] + [last_inbox.at[k, i] for i in (1, 3, 5)]).astype(jnp.bfloat16)
        last_start(k, last_zout.at[pl.ds(k, 1)], lands(ACROSS, k)[0], across, ACROSS)

    def early_over_z(k):
        last_start(k, last_part.at[k, pl.ds(XSIDE, XSIDE)], 0, across, ACROSS)

    def late_send_parts(k):
        last_arrived(ACROSS, k)
        for d, device in beyond:
            last_sums[k - 2, d - 1] = add(last_part.at[k, d], last_inbox.at[k, d]).astype(jnp.bfloat16)
            last_start(k, last_sums.at[k - 2, pl.ds(d - 1, 1)], lands(PARTS, k)[0] + d - 1, device, PARTS)

    def last_encode(k):
        last_arrived(ACROSS if k < 2 else PARTS, k)
        gradient = add(*[last_part.at[k, 0]] + [last_inbox.at[k, i] for i in ((0, 2, 4, 6) if k < 2 else (0, 4, 5, 6))])
        c, columns = place_of(k)
        last_gout[k] = code(c, columns, gradient)
        first = lands(GOSSIP, k)[0]
        last_start(k, last_gout.at[pl.ds(k, 1)], first, far, GOSSIP)
        last_start(k, last_gout.at[pl.ds(k, 1)], first + 1, near, GOSSIP)

    def last_update(k):
        last_arrived(GOSSIP, k)
        c, columns = place_of(k)
        first = lands(GOSSIP, k)[0]
        params, public, mixed = mix_in(c, columns, add(last_inbox.at[k, first], last_inbox.at[k, first + 1]))
        there = pl.ds(c * w + columns.start, wl)
        opar[0, :, there] = params
        opub[0, :, there] = public
        omix[0, :, there] = mixed

    block = lax.broadcasted_iota(jnp.int32, pool.shape, 0) % LANES // BLOCK
    lane_block = lax.broadcasted_iota(jnp.int32, pool.shape, 1) // BLOCK

    hid_load.wait()
    hid_t[0] = hid[0].T
    multiply(0)
    pl.semaphore_wait(barrier, 6)
    send_parts(0)

    for t in (*range(1, AHEAD), items + 1, items):
        cot_load(t).start()

    @pl.loop(AHEAD, items)
    def _(t):
        cot_load(t).start()

    @pl.loop(0, chunks)
    def _(c):
        for copy in state_loads(c):
            copy.start()

    for t in range(1, AHEAD):
        multiply(t)
        send_parts(t)
    for r in range(1, rounds):
        hid_t[r] = hid[r].T
    pool[...] = (block == lane_block).astype(jnp.bfloat16)

    multiply_last(1)
    early_over_z(2)
    early_over_z(3)

    for t in range(AHEAD, EARLY):
        multiply(t)

    def stage(work, item):
        @pl.when((item >= 0) & (item < items))
        def _():
            work(item)

    late = {2: ((multiply_last, 0),), items - 3: ((last_send_parts, 0),), items - 2: ((last_send_parts, 1),),
            items - 1: ((late_send_parts, 2), (late_send_parts, 3)),
            items: ((last_over_z, 0),), items + 1: ((last_over_z, 1), (last_encode, 2), (last_encode, 3)),
            items + 3: ((last_encode, 0), (last_encode, 1)),
            items + 5: ((last_update, 2), (last_update, 3), (last_update, 0), (last_update, 1))}

    @pl.loop(0, items + LAGS[-1])
    def _(t):
        stage(pass_on, t)
        stage(send_parts, t + AHEAD)
        stage(over_z, t - LAGS[0])
        for step, works in late.items():
            @pl.when(t == step)
            def _():
                for work, k in works:
                    work(k)
        stage(encode, t - LAGS[1])
        stage(update, t - LAGS[2])
        stage(multiply, t + EARLY)

    pltpu.make_async_copy(inbox, inbox, send_sem.at[0]).wait()
    pltpu.make_async_copy(last_inbox, last_inbox, send_sem.at[1]).wait()


def deliver(*refs):
    sem = refs[-1]
    arrays = (len(refs) - 1) // 2
    copies = []
    for i in range(arrays):
        half = refs[i].shape[1] // 2
        for j in range(2):
            piece = (0, pl.ds(j * half, half))
            copies.append(pltpu.make_async_copy(refs[i].at[piece], refs[arrays + i].at[piece], sem.at[i, j]))
    for copy in copies:
        copy.start()
    for copy in copies:
        copy.wait()


def per_device(params, public, mixed, hidden, cotangent):
    _, rows, width = params.shape
    _, rounds, tokens, rows_all = hidden.shape
    items = rounds * CHUNKS - 2
    w = width // CHUNKS
    piece = pltpu.VMEM((items, rows, w), jnp.bfloat16)
    state = pltpu.VMEM((CHUNKS, rows, w), jnp.float32)
    anywhere = pl.BlockSpec(memory_space=pl.ANY)
    in_vmem = pl.BlockSpec(memory_space=pltpu.VMEM)
    results = pl.pallas_call(
        kernel,
        out_shape=(pltpu.VMEM(params.shape, jnp.float32),) * 3,
        in_specs=[anywhere] * 5,
        out_specs=(in_vmem,) * 3,
        scratch_shapes=[
            pltpu.VMEM((rounds, tokens, rows_all), jnp.bfloat16),
            pltpu.VMEM((rounds, rows_all, tokens), jnp.bfloat16),
            pltpu.VMEM((items + 2, tokens, w), jnp.bfloat16),
            state, state, state,
            pltpu.VMEM((items, rows_all // rows, rows, w), jnp.bfloat16),
            pltpu.VMEM((items, INBOX, rows, w), jnp.bfloat16),
            *[piece] * 4,
            state, state,
            pltpu.VMEM((2 * LANES, LANES), jnp.bfloat16),
            pltpu.VMEM((PIECES, rows_all // rows, rows, w // 2), jnp.bfloat16),
            pltpu.VMEM((PIECES, INBOX, rows, w // 2), jnp.bfloat16),
            pltpu.VMEM((2, rows, w // 2), jnp.bfloat16),
            pltpu.VMEM((2, XSIDE - 1, rows, w // 2), jnp.bfloat16),
            pltpu.VMEM((PIECES, rows, w // 2), jnp.bfloat16),
            pltpu.SemaphoreType.DMA((5,)),
            pltpu.SemaphoreType.DMA((items + 2,)),
            pltpu.SemaphoreType.DMA((3, CHUNKS)),
            pltpu.SemaphoreType.DMA((2,)),
            pltpu.SemaphoreType.DMA((len(LANDS), items)),
            pltpu.SemaphoreType.DMA((len(LANDS), PIECES)),
        ],
        compiler_params=pltpu.CompilerParams(
            collective_id=0, has_side_effects=True, vmem_limit_bytes=40 * 1024 * 1024),
        cost_estimate=pl.CostEstimate(flops=340_000_000, bytes_accessed=5_000_000, transcendentals=0),
    )(*[pltpu.with_memory_space_constraint(a, pltpu.HBM) for a in (params, public, mixed, hidden, cotangent)])
    return pl.pallas_call(
        deliver,
        out_shape=(jax.ShapeDtypeStruct(params.shape, jnp.float32),) * 3,
        in_specs=[in_vmem] * 3,
        out_specs=(anywhere,) * 3,
        scratch_shapes=[pltpu.SemaphoreType.DMA((3, 2))],
        compiler_params=pltpu.CompilerParams(vmem_limit_bytes=1024 * 1024),
    )(*[pltpu.with_memory_space_constraint(a, pltpu.VMEM) for a in results])


def solution(mesh):
    state = P("blk", "fsdp", None)
    tokens = P("blk", None, "fsdp", None)
    return jax.shard_map(
        per_device,
        mesh=mesh,
        in_specs=(state, state, state, tokens, tokens),
        out_specs=(state, state, state),
        check_vma=False,
    )
```

```python
import functools

import jax
import jax.numpy as jnp
from jax import lax
from jax.experimental import pallas as pl
from jax.experimental.pallas import tpu as pltpu
from jax.sharding import PartitionSpec as P

MESH = pl.DeviceIdType.MESH
BLOCK = 32
LANES = 128
LEARN_RATE = 0.25
MIX_RATE = 0.4
SCALE_FLOOR = 0.25
CODE_LIMIT = 2.0
CHUNKS = 5
XSIDE = 4
AHEAD = 3
EARLY = 5
LAGS = (2, 4, 6)

TO_RIGHT, TO_LEFT, SUM_O, SUM_M, OVER, GO_FAR, GO_NEAR = range(7)
PARTS, SUMS, ACROSS, GOSSIP = range(4)
LANDS = ((0, 4), (4, 2), (6, 1), (7, 2))
INBOX = 9
NEAR_M, FAR_O, FAR_M, NEAR_O, IN_SUM_O, IN_SUM_M, IN_ACROSS, IN_FAR, IN_NEAR = range(INBOX)

PIECES = 4
LANDS_X_FIRST = {PARTS: (0, 6), ACROSS: (6, 1), GOSSIP: (7, 2)}
LANDS_Z_FIRST = {ACROSS: (0, 4), PARTS: (4, 3), GOSSIP: (7, 2)}

OWN_MINE, NEXT_OTHER, LAST_MINE, OWN_OTHER = 0, 1, 2, 3
LEFT_PAIR, RIGHT_PAIR = 4, 6


def tall(wide):
    n = wide.shape[1] // LANES
    return jnp.concatenate([wide[:, i * LANES:(i + 1) * LANES] for i in range(n)], axis=0)


def flat(high, rows):
    n = high.shape[0] // rows
    return jnp.concatenate([high[i * rows:(i + 1) * rows] for i in range(n)], axis=1)


def add(*refs):
    total = refs[0][...].astype(jnp.float32)
    for ref in refs[1:]:
        total = total + ref[...].astype(jnp.float32)
    return total


def kernel(par_hbm, pub_hbm, mix_hbm, hid_hbm, cot_hbm, opar, opub, omix,
           hid, hid_t, cot, par, pub, mix, part, inbox, fwd_o, fwd_m, zout, gout, step_v, mess_v, pool,
           last_part, last_inbox, last_zout, last_sums, last_gout,
           hid_sem, cot_sem, state_sem, send_sem, recv_sem, last_recv_sem):
    rounds, tokens, rows_all = hid.shape
    chunks, rows, w = par.shape
    items = rounds * chunks - 2
    wl = w // 2

    b = lax.axis_index("blk")
    f = lax.axis_index("fsdp")
    nb = lax.axis_size("blk")
    x, zh = f // 2, f % 2
    right = (b, (x + 1) % XSIDE * 2 + zh)
    left = (b, (x + XSIDE - 1) % XSIDE * 2 + zh)
    across = (b, x * 2 + 1 - zh)
    opposite = (b, (x + 2) % XSIDE * 2 + zh)
    core = b % 2
    far = ((b + nb - 1 + 2 * core) % nb, f)
    near = (b + 1 - 2 * core, f)

    def cols(c):
        return pl.ds(pl.multiple_of(c * w, LANES), w)

    def chunk_of(t):
        if isinstance(t, int) and t >= items:
            return 1 - (t - items)
        return t - t // chunks * (chunks - 2)

    hid_load = pltpu.make_async_copy(hid_hbm.at[0], hid, hid_sem.at[0])

    def cot_load(t):
        return pltpu.make_async_copy(cot_hbm.at[0, t // chunks, :, cols(chunk_of(t))], cot.at[t], cot_sem.at[t])

    def state_loads(c):
        return [pltpu.make_async_copy(src.at[0, :, cols(c)], dst.at[c], state_sem.at[i, c])
                for i, (src, dst) in enumerate(((par_hbm, par), (pub_hbm, pub), (mix_hbm, mix)))]

    def first_loads():
        step = tokens // 4
        return [pltpu.make_async_copy(cot_hbm.at[0, 0, pl.ds(i * step, step), pl.ds(0, w)],
                                      cot.at[0, pl.ds(i * step, step)], hid_sem.at[1 + i]) for i in range(4)]

    hid_load.start()
    for copy in first_loads():
        copy.start()

    barrier = pltpu.get_barrier_semaphore()
    for device in (right, left, opposite, across, far, near):
        pl.semaphore_signal(barrier, inc=1, device_id=device, device_id_type=MESH)

    def land(t, first, blocks=1):
        return inbox.at[t, pl.ds(first, blocks)]

    def start(kind, t):
        src, dst, device, group = {
            TO_RIGHT: lambda: (part.at[t, pl.ds(RIGHT_PAIR, 2)], land(t, NEAR_M, 2), right, PARTS),
            TO_LEFT: lambda: (part.at[t, pl.ds(LEFT_PAIR, 2)], land(t, FAR_M, 2), left, PARTS),
            SUM_O: lambda: (fwd_o.at[pl.ds(t, 1)], land(t, IN_SUM_O), right, SUMS),
            SUM_M: lambda: (fwd_m.at[pl.ds(t, 1)], land(t, IN_SUM_M), left, SUMS),
            OVER: lambda: (zout.at[pl.ds(t, 1)], land(t, IN_ACROSS), across, ACROSS),
            GO_FAR: lambda: (gout.at[pl.ds(t, 1)], land(t, IN_FAR), far, GOSSIP),
            GO_NEAR: lambda: (gout.at[pl.ds(t, 1)], land(t, IN_NEAR), near, GOSSIP),
        }[kind]()
        pltpu.make_async_remote_copy(
            src_ref=src, dst_ref=dst, send_sem=send_sem.at[0], recv_sem=recv_sem.at[group, t],
            device_id=device, device_id_type=MESH).start()

    def arrived(group, t):
        blocks = land(t, *LANDS[group])
        pltpu.make_async_copy(blocks, blocks, recv_sem.at[group, t]).wait()

    places = [3 * ((j // 2 + XSIDE - x) % XSIDE * 2 + (j + zh) % 2) % 8 for j in range(rows_all // rows)]

    def product(t):
        if not isinstance(t, int) or t > 0:
            cot_load(t).wait()
        else:
            for copy in first_loads():
                copy.wait()
        return jnp.dot(hid_t[t // chunks], cot[t], preferred_element_type=jnp.float32).astype(jnp.bfloat16)

    def multiply(t):
        blocks = product(t)
        for j, place in enumerate(places):
            part[t, place] = blocks[j * rows:(j + 1) * rows]

    def multiply_last(pair):
        blocks = product(items + pair)
        for j, place in enumerate(places):
            which = place * 3 % 8
            if pair == 1:
                which = which % 2 * XSIDE + which // 2
            for i in range(2):
                last_part[2 * pair + i, which] = blocks[j * rows:(j + 1) * rows, i * wl:(i + 1) * wl]

    def send_parts(t):
        start(TO_RIGHT, t)
        start(TO_LEFT, t)

    def pass_on(t):
        arrived(PARTS, t)
        fwd_o[t] = add(inbox.at[t, FAR_O], part.at[t, NEXT_OTHER]).astype(jnp.bfloat16)
        start(SUM_O, t)
        fwd_m[t] = add(inbox.at[t, FAR_M], part.at[t, LAST_MINE]).astype(jnp.bfloat16)
        start(SUM_M, t)

    def over_z(t):
        arrived(SUMS, t)
        zout[t] = add(part.at[t, OWN_OTHER], inbox.at[t, NEAR_O], inbox.at[t, IN_SUM_O]).astype(jnp.bfloat16)
        start(OVER, t)

    def code(c, columns, gradient):
        stepped = par[c, :, columns] - LEARN_RATE * gradient
        public = pub[c, :, columns]
        change = tall(stepped - public)
        square = change * change
        high = square.astype(jnp.bfloat16)
        low = (square - high.astype(jnp.float32)).astype(jnp.bfloat16)
        energy = jnp.dot(jnp.concatenate([high, low], axis=1), pool[...], preferred_element_type=jnp.float32)
        scales = jnp.maximum(jnp.sqrt(energy * (1.0 / BLOCK)), SCALE_FLOOR).astype(jnp.bfloat16)
        wide = scales.astype(jnp.float32)
        coded = jnp.clip(change / wide, -CODE_LIMIT, CODE_LIMIT).astype(jnp.bfloat16)
        message = flat(coded.astype(jnp.float32) * wide, rows)
        pub[c, :, columns] = public + message
        step_v[c, :, columns] = stepped
        mess_v[c, :, columns] = message
        return message.astype(jnp.bfloat16)

    def mix_in(c, columns, heard):
        public = pub[c, :, columns]
        mixed = mix[c, :, columns] + (mess_v[c, :, columns] + heard) * (1.0 / 3.0)
        return step_v[c, :, columns] + MIX_RATE * (mixed - public), public, mixed

    def encode(t):
        c = chunk_of(t)

        @pl.when(t < chunks)
        def _():
            for copy in state_loads(c):
                copy.wait()

        arrived(ACROSS, t)
        gradient = add(part.at[t, OWN_MINE], inbox.at[t, NEAR_M], inbox.at[t, IN_SUM_M], inbox.at[t, IN_ACROSS])
        gout[t] = code(c, slice(0, w), gradient)
        start(GO_FAR, t)
        start(GO_NEAR, t)

    def update(t):
        c = chunk_of(t)
        arrived(GOSSIP, t)
        params, public, mixed = mix_in(c, slice(0, w), add(inbox.at[t, IN_FAR], inbox.at[t, IN_NEAR]))

        @pl.when(t < (rounds - 1) * chunks)
        def _():
            mix[c] = mixed
            par[c] = params

        @pl.when(t >= (rounds - 1) * chunks)
        def _():
            opar[0, :, cols(c)] = params
            opub[0, :, cols(c)] = public
            omix[0, :, cols(c)] = mixed

    def lands(group, k):
        return (LANDS_X_FIRST if k < 2 else LANDS_Z_FIRST)[group]

    def place_of(k):
        return 1 - k // 2, slice(k % 2 * wl, k % 2 * wl + wl)

    def last_start(k, src, slot, device, group):
        pltpu.make_async_remote_copy(
            src_ref=src, dst_ref=last_inbox.at[k, pl.ds(slot, src.shape[0])], send_sem=send_sem.at[1],
            recv_sem=last_recv_sem.at[group, k], device_id=device, device_id_type=MESH).start()

    def last_arrived(group, k):
        first, blocks = lands(group, k)
        blocks = last_inbox.at[k, pl.ds(first, blocks)]
        pltpu.make_async_copy(blocks, blocks, last_recv_sem.at[group, k]).wait()

    beyond = ((2, opposite), (1, right), (3, left))

    def last_send_parts(k):
        for d, device in beyond:
            last_start(k, last_part.at[k, pl.ds(2 * d, 2)], 2 * d - 2, device, PARTS)

    def last_over_z(k):
        last_arrived(PARTS, k)
        last_zout[k] = add(*[last_part.at[k, 1]] + [last_inbox.at[k, i] for i in (1, 3, 5)]).astype(jnp.bfloat16)
        last_start(k, last_zout.at[pl.ds(k, 1)], lands(ACROSS, k)[0], across, ACROSS)

    def early_over_z(k):
        last_start(k, last_part.at[k, pl.ds(XSIDE, XSIDE)], 0, across, ACROSS)

    def late_send_parts(k):
        last_arrived(ACROSS, k)
        for d, device in beyond:
            last_sums[k - 2, d - 1] = add(last_part.at[k, d], last_inbox.at[k, d]).astype(jnp.bfloat16)
            last_start(k, last_sums.at[k - 2, pl.ds(d - 1, 1)], lands(PARTS, k)[0] + d - 1, device, PARTS)

    def last_encode(k):
        last_arrived(ACROSS if k < 2 else PARTS, k)
        gradient = add(*[last_part.at[k, 0]] + [last_inbox.at[k, i] for i in ((0, 2, 4, 6) if k < 2 else (0, 4, 5, 6))])
        c, columns = place_of(k)
        last_gout[k] = code(c, columns, gradient)
        first = lands(GOSSIP, k)[0]
        last_start(k, last_gout.at[pl.ds(k, 1)], first, far, GOSSIP)
        last_start(k, last_gout.at[pl.ds(k, 1)], first + 1, near, GOSSIP)

    def last_update(k):
        last_arrived(GOSSIP, k)
        c, columns = place_of(k)
        first = lands(GOSSIP, k)[0]
        params, public, mixed = mix_in(c, columns, add(last_inbox.at[k, first], last_inbox.at[k, first + 1]))
        there = pl.ds(c * w + columns.start, wl)
        opar[0, :, there] = params
        opub[0, :, there] = public
        omix[0, :, there] = mixed

    block = lax.broadcasted_iota(jnp.int32, pool.shape, 0) % LANES // BLOCK
    lane_block = lax.broadcasted_iota(jnp.int32, pool.shape, 1) // BLOCK

    hid_load.wait()
    hid_t[0] = hid[0].T
    multiply(0)
    pl.semaphore_wait(barrier, 6)
    send_parts(0)

    for t in (*range(1, AHEAD), items + 1, items):
        cot_load(t).start()

    @pl.loop(AHEAD, items)
    def _(t):
        cot_load(t).start()

    @pl.loop(0, chunks)
    def _(c):
        for copy in state_loads(c):
            copy.start()

    for t in range(1, AHEAD):
        multiply(t)
        send_parts(t)
    for r in range(1, rounds):
        hid_t[r] = hid[r].T
    pool[...] = (block == lane_block).astype(jnp.bfloat16)

    multiply_last(1)
    early_over_z(2)
    early_over_z(3)

    for t in range(AHEAD, EARLY):
        multiply(t)

    def stage(work, item):
        @pl.when((item >= 0) & (item < items))
        def _():
            work(item)

    late = {2: ((multiply_last, 0),), items - 3: ((last_send_parts, 0),),
            items - 1: ((last_send_parts, 1), (late_send_parts, 2), (late_send_parts, 3)),
            items: ((last_over_z, 0),), items + 1: ((last_over_z, 1), (last_encode, 2), (last_encode, 3)),
            items + 3: ((last_encode, 0),), items + 4: ((last_encode, 1),),
            items + 5: ((last_update, 2), (last_update, 3), (last_update, 0), (last_update, 1))}

    @pl.loop(0, items + LAGS[-1])
    def _(t):
        stage(pass_on, t)
        stage(send_parts, t + AHEAD)
        stage(over_z, t - LAGS[0])
        for step, works in late.items():
            @pl.when(t == step)
            def _():
                for work, k in works:
                    work(k)
        stage(encode, t - LAGS[1])
        stage(update, t - LAGS[2])
        stage(multiply, t + EARLY)

    pltpu.make_async_copy(inbox, inbox, send_sem.at[0]).wait()
    pltpu.make_async_copy(last_inbox, last_inbox, send_sem.at[1]).wait()


def deliver(*refs):
    sem = refs[-1]
    arrays = (len(refs) - 1) // 2
    copies = []
    for i in range(arrays):
        half = refs[i].shape[1] // 2
        for j in range(2):
            piece = (0, pl.ds(j * half, half))
            copies.append(pltpu.make_async_copy(refs[i].at[piece], refs[arrays + i].at[piece], sem.at[i, j]))
    for copy in copies:
        copy.start()
    for copy in copies:
        copy.wait()


def per_device(params, public, mixed, hidden, cotangent):
    _, rows, width = params.shape
    _, rounds, tokens, rows_all = hidden.shape
    items = rounds * CHUNKS - 2
    w = width // CHUNKS
    piece = pltpu.VMEM((items, rows, w), jnp.bfloat16)
    state = pltpu.VMEM((CHUNKS, rows, w), jnp.float32)
    anywhere = pl.BlockSpec(memory_space=pl.ANY)
    in_vmem = pl.BlockSpec(memory_space=pltpu.VMEM)
    results = pl.pallas_call(
        kernel,
        out_shape=(pltpu.VMEM(params.shape, jnp.float32),) * 3,
        in_specs=[anywhere] * 5,
        out_specs=(in_vmem,) * 3,
        scratch_shapes=[
            pltpu.VMEM((rounds, tokens, rows_all), jnp.bfloat16),
            pltpu.VMEM((rounds, rows_all, tokens), jnp.bfloat16),
            pltpu.VMEM((items + 2, tokens, w), jnp.bfloat16),
            state, state, state,
            pltpu.VMEM((items, rows_all // rows, rows, w), jnp.bfloat16),
            pltpu.VMEM((items, INBOX, rows, w), jnp.bfloat16),
            *[piece] * 4,
            state, state,
            pltpu.VMEM((2 * LANES, LANES), jnp.bfloat16),
            pltpu.VMEM((PIECES, rows_all // rows, rows, w // 2), jnp.bfloat16),
            pltpu.VMEM((PIECES, INBOX, rows, w // 2), jnp.bfloat16),
            pltpu.VMEM((2, rows, w // 2), jnp.bfloat16),
            pltpu.VMEM((2, XSIDE - 1, rows, w // 2), jnp.bfloat16),
            pltpu.VMEM((PIECES, rows, w // 2), jnp.bfloat16),
            pltpu.SemaphoreType.DMA((5,)),
            pltpu.SemaphoreType.DMA((items + 2,)),
            pltpu.SemaphoreType.DMA((3, CHUNKS)),
            pltpu.SemaphoreType.DMA((2,)),
            pltpu.SemaphoreType.DMA((len(LANDS), items)),
            pltpu.SemaphoreType.DMA((len(LANDS), PIECES)),
        ],
        compiler_params=pltpu.CompilerParams(
            collective_id=0, has_side_effects=True, vmem_limit_bytes=40 * 1024 * 1024),
        cost_estimate=pl.CostEstimate(flops=340_000_000, bytes_accessed=5_000_000, transcendentals=0),
    )(*[pltpu.with_memory_space_constraint(a, pltpu.HBM) for a in (params, public, mixed, hidden, cotangent)])
    return pl.pallas_call(
        deliver,
        out_shape=(jax.ShapeDtypeStruct(params.shape, jnp.float32),) * 3,
        in_specs=[in_vmem] * 3,
        out_specs=(anywhere,) * 3,
        scratch_shapes=[pltpu.SemaphoreType.DMA((3, 2))],
        compiler_params=pltpu.CompilerParams(vmem_limit_bytes=1024 * 1024),
    )(*[pltpu.with_memory_space_constraint(a, pltpu.VMEM) for a in results])


def solution(mesh):
    state = P("blk", "fsdp", None)
    tokens = P("blk", None, "fsdp", None)
    return jax.shard_map(
        per_device,
        mesh=mesh,
        in_specs=(state, state, state, tokens, tokens),
        out_specs=(state, state, state),
        check_vma=False,
    )
```

```python
import functools

import jax
import jax.numpy as jnp
from jax import lax
from jax.experimental import pallas as pl
from jax.experimental.pallas import tpu as pltpu
from jax.sharding import PartitionSpec as P

MESH = pl.DeviceIdType.MESH
BLOCK = 32
LANES = 128
LEARN_RATE = 0.25
MIX_RATE = 0.4
SCALE_FLOOR = 0.25
CODE_LIMIT = 2.0
CHUNKS = 5
XSIDE = 4
AHEAD = 4
EARLY = 5
LAGS = (2, 4, 6)

TO_RIGHT, TO_LEFT, SUM_O, SUM_M, OVER, GO_FAR, GO_NEAR = range(7)
PARTS, SUMS, ACROSS, GOSSIP = range(4)
LANDS = ((0, 4), (4, 2), (6, 1), (7, 2))
INBOX = 9
NEAR_M, FAR_O, FAR_M, NEAR_O, IN_SUM_O, IN_SUM_M, IN_ACROSS, IN_FAR, IN_NEAR = range(INBOX)

PIECES = 4
LANDS_X_FIRST = {PARTS: (0, 6), ACROSS: (6, 1), GOSSIP: (7, 2)}
LANDS_Z_FIRST = {ACROSS: (0, 4), PARTS: (4, 3), GOSSIP: (7, 2)}

OWN_MINE, NEXT_OTHER, LAST_MINE, OWN_OTHER = 0, 1, 2, 3
LEFT_PAIR, RIGHT_PAIR = 4, 6


def tall(wide):
    n = wide.shape[1] // LANES
    return jnp.concatenate([wide[:, i * LANES:(i + 1) * LANES] for i in range(n)], axis=0)


def flat(high, rows):
    n = high.shape[0] // rows
    return jnp.concatenate([high[i * rows:(i + 1) * rows] for i in range(n)], axis=1)


def add(*refs):
    total = refs[0][...].astype(jnp.float32)
    for ref in refs[1:]:
        total = total + ref[...].astype(jnp.float32)
    return total


def kernel(par_hbm, pub_hbm, mix_hbm, hid_hbm, cot_hbm, opar, opub, omix,
           hid, hid_t, cot, par, pub, mix, part, inbox, fwd_o, fwd_m, zout, gout, step_v, mess_v, pool,
           last_part, last_inbox, last_zout, last_sums, last_gout,
           hid_sem, cot_sem, state_sem, send_sem, recv_sem, last_recv_sem):
    rounds, tokens, rows_all = hid.shape
    chunks, rows, w = par.shape
    items = rounds * chunks - 2
    wl = w // 2

    b = lax.axis_index("blk")
    f = lax.axis_index("fsdp")
    nb = lax.axis_size("blk")
    x, zh = f // 2, f % 2
    right = (b, (x + 1) % XSIDE * 2 + zh)
    left = (b, (x + XSIDE - 1) % XSIDE * 2 + zh)
    across = (b, x * 2 + 1 - zh)
    opposite = (b, (x + 2) % XSIDE * 2 + zh)
    core = b % 2
    far = ((b + nb - 1 + 2 * core) % nb, f)
    near = (b + 1 - 2 * core, f)

    def cols(c):
        return pl.ds(pl.multiple_of(c * w, LANES), w)

    def chunk_of(t):
        if isinstance(t, int) and t >= items:
            return 1 - (t - items)
        return t - t // chunks * (chunks - 2)

    hid_load = pltpu.make_async_copy(hid_hbm.at[0], hid, hid_sem.at[0])

    def cot_load(t):
        return pltpu.make_async_copy(cot_hbm.at[0, t // chunks, :, cols(chunk_of(t))], cot.at[t], cot_sem.at[t])

    def state_loads(c):
        return [pltpu.make_async_copy(src.at[0, :, cols(c)], dst.at[c], state_sem.at[i, c])
                for i, (src, dst) in enumerate(((par_hbm, par), (pub_hbm, pub), (mix_hbm, mix)))]

    def first_loads():
        step = tokens // 4
        return [pltpu.make_async_copy(cot_hbm.at[0, 0, pl.ds(i * step, step), pl.ds(0, w)],
                                      cot.at[0, pl.ds(i * step, step)], hid_sem.at[1 + i]) for i in range(4)]

    hid_load.start()
    for copy in first_loads():
        copy.start()

    barrier = pltpu.get_barrier_semaphore()
    for device in (right, left, opposite, across, far, near):
        pl.semaphore_signal(barrier, inc=1, device_id=device, device_id_type=MESH)

    def land(t, first, blocks=1):
        return inbox.at[t, pl.ds(first, blocks)]

    def start(kind, t):
        src, dst, device, group = {
            TO_RIGHT: lambda: (part.at[t, pl.ds(RIGHT_PAIR, 2)], land(t, NEAR_M, 2), right, PARTS),
            TO_LEFT: lambda: (part.at[t, pl.ds(LEFT_PAIR, 2)], land(t, FAR_M, 2), left, PARTS),
            SUM_O: lambda: (fwd_o.at[pl.ds(t, 1)], land(t, IN_SUM_O), right, SUMS),
            SUM_M: lambda: (fwd_m.at[pl.ds(t, 1)], land(t, IN_SUM_M), left, SUMS),
            OVER: lambda: (zout.at[pl.ds(t, 1)], land(t, IN_ACROSS), across, ACROSS),
            GO_FAR: lambda: (gout.at[pl.ds(t, 1)], land(t, IN_FAR), far, GOSSIP),
            GO_NEAR: lambda: (gout.at[pl.ds(t, 1)], land(t, IN_NEAR), near, GOSSIP),
        }[kind]()
        pltpu.make_async_remote_copy(
            src_ref=src, dst_ref=dst, send_sem=send_sem.at[0], recv_sem=recv_sem.at[group, t],
            device_id=device, device_id_type=MESH).start()

    def arrived(group, t):
        blocks = land(t, *LANDS[group])
        pltpu.make_async_copy(blocks, blocks, recv_sem.at[group, t]).wait()

    places = [3 * ((j // 2 + XSIDE - x) % XSIDE * 2 + (j + zh) % 2) % 8 for j in range(rows_all // rows)]

    def product(t):
        if not isinstance(t, int) or t > 0:
            cot_load(t).wait()
        else:
            for copy in first_loads():
                copy.wait()
        return jnp.dot(hid_t[t // chunks], cot[t], preferred_element_type=jnp.float32).astype(jnp.bfloat16)

    def multiply(t):
        blocks = product(t)
        for j, place in enumerate(places):
            part[t, place] = blocks[j * rows:(j + 1) * rows]

    def multiply_last(pair):
        blocks = product(items + pair)
        for j, place in enumerate(places):
            which = place * 3 % 8
            if pair == 1:
                which = which % 2 * XSIDE + which // 2
            for i in range(2):
                last_part[2 * pair + i, which] = blocks[j * rows:(j + 1) * rows, i * wl:(i + 1) * wl]

    def send_parts(t):
        start(TO_RIGHT, t)
        start(TO_LEFT, t)

    def pass_on(t):
        arrived(PARTS, t)
        fwd_o[t] = add(inbox.at[t, FAR_O], part.at[t, NEXT_OTHER]).astype(jnp.bfloat16)
        start(SUM_O, t)
        fwd_m[t] = add(inbox.at[t, FAR_M], part.at[t, LAST_MINE]).astype(jnp.bfloat16)
        start(SUM_M, t)

    def over_z(t):
        arrived(SUMS, t)
        zout[t] = add(part.at[t, OWN_OTHER], inbox.at[t, NEAR_O], inbox.at[t, IN_SUM_O]).astype(jnp.bfloat16)
        start(OVER, t)

    def code(c, columns, gradient):
        stepped = par[c, :, columns] - LEARN_RATE * gradient
        public = pub[c, :, columns]
        change = tall(stepped - public)
        square = change * change
        high = square.astype(jnp.bfloat16)
        low = (square - high.astype(jnp.float32)).astype(jnp.bfloat16)
        energy = jnp.dot(jnp.concatenate([high, low], axis=1), pool[...], preferred_element_type=jnp.float32)
        scales = jnp.maximum(jnp.sqrt(energy * (1.0 / BLOCK)), SCALE_FLOOR).astype(jnp.bfloat16)
        wide = scales.astype(jnp.float32)
        coded = jnp.clip(change / wide, -CODE_LIMIT, CODE_LIMIT).astype(jnp.bfloat16)
        message = flat(coded.astype(jnp.float32) * wide, rows)
        pub[c, :, columns] = public + message
        step_v[c, :, columns] = stepped
        mess_v[c, :, columns] = message
        return message.astype(jnp.bfloat16)

    def mix_in(c, columns, heard):
        public = pub[c, :, columns]
        mixed = mix[c, :, columns] + (mess_v[c, :, columns] + heard) * (1.0 / 3.0)
        return step_v[c, :, columns] + MIX_RATE * (mixed - public), public, mixed

    def encode(t):
        c = chunk_of(t)

        @pl.when(t < chunks)
        def _():
            for copy in state_loads(c):
                copy.wait()

        arrived(ACROSS, t)
        gradient = add(part.at[t, OWN_MINE], inbox.at[t, NEAR_M], inbox.at[t, IN_SUM_M], inbox.at[t, IN_ACROSS])
        gout[t] = code(c, slice(0, w), gradient)
        start(GO_FAR, t)
        start(GO_NEAR, t)

    def update(t):
        c = chunk_of(t)
        arrived(GOSSIP, t)
        params, public, mixed = mix_in(c, slice(0, w), add(inbox.at[t, IN_FAR], inbox.at[t, IN_NEAR]))

        @pl.when(t < (rounds - 1) * chunks)
        def _():
            mix[c] = mixed
            par[c] = params

        @pl.when(t >= (rounds - 1) * chunks)
        def _():
            opar[0, :, cols(c)] = params
            opub[0, :, cols(c)] = public
            omix[0, :, cols(c)] = mixed

    def lands(group, k):
        return (LANDS_X_FIRST if k < 2 else LANDS_Z_FIRST)[group]

    def place_of(k):
        return 1 - k // 2, slice(k % 2 * wl, k % 2 * wl + wl)

    def last_start(k, src, slot, device, group):
        pltpu.make_async_remote_copy(
            src_ref=src, dst_ref=last_inbox.at[k, pl.ds(slot, src.shape[0])], send_sem=send_sem.at[1],
            recv_sem=last_recv_sem.at[group, k], device_id=device, device_id_type=MESH).start()

    def last_arrived(group, k):
        first, blocks = lands(group, k)
        blocks = last_inbox.at[k, pl.ds(first, blocks)]
        pltpu.make_async_copy(blocks, blocks, last_recv_sem.at[group, k]).wait()

    beyond = ((2, opposite), (1, right), (3, left))

    def last_send_parts(k):
        for d, device in beyond:
            last_start(k, last_part.at[k, pl.ds(2 * d, 2)], 2 * d - 2, device, PARTS)

    def last_over_z(k):
        last_arrived(PARTS, k)
        last_zout[k] = add(*[last_part.at[k, 1]] + [last_inbox.at[k, i] for i in (1, 3, 5)]).astype(jnp.bfloat16)
        last_start(k, last_zout.at[pl.ds(k, 1)], lands(ACROSS, k)[0], across, ACROSS)

    def early_over_z(k):
        last_start(k, last_part.at[k, pl.ds(XSIDE, XSIDE)], 0, across, ACROSS)

    def late_send_parts(k):
        last_arrived(ACROSS, k)
        for d, device in beyond:
            last_sums[k - 2, d - 1] = add(last_part.at[k, d], last_inbox.at[k, d]).astype(jnp.bfloat16)
            last_start(k, last_sums.at[k - 2, pl.ds(d - 1, 1)], lands(PARTS, k)[0] + d - 1, device, PARTS)

    def last_encode(k):
        last_arrived(ACROSS if k < 2 else PARTS, k)
        gradient = add(*[last_part.at[k, 0]] + [last_inbox.at[k, i] for i in ((0, 2, 4, 6) if k < 2 else (0, 4, 5, 6))])
        c, columns = place_of(k)
        last_gout[k] = code(c, columns, gradient)
        first = lands(GOSSIP, k)[0]
        last_start(k, last_gout.at[pl.ds(k, 1)], first, far, GOSSIP)
        last_start(k, last_gout.at[pl.ds(k, 1)], first + 1, near, GOSSIP)

    def last_update(k):
        last_arrived(GOSSIP, k)
        c, columns = place_of(k)
        first = lands(GOSSIP, k)[0]
        params, public, mixed = mix_in(c, columns, add(last_inbox.at[k, first], last_inbox.at[k, first + 1]))
        there = pl.ds(c * w + columns.start, wl)
        opar[0, :, there] = params
        opub[0, :, there] = public
        omix[0, :, there] = mixed

    block = lax.broadcasted_iota(jnp.int32, pool.shape, 0) % LANES // BLOCK
    lane_block = lax.broadcasted_iota(jnp.int32, pool.shape, 1) // BLOCK

    hid_load.wait()
    hid_t[0] = hid[0].T
    multiply(0)
    pl.semaphore_wait(barrier, 6)
    send_parts(0)

    for t in (*range(1, AHEAD), items + 1, items):
        cot_load(t).start()

    @pl.loop(AHEAD, items)
    def _(t):
        cot_load(t).start()

    @pl.loop(0, chunks)
    def _(c):
        for copy in state_loads(c):
            copy.start()

    for t in range(1, AHEAD):
        multiply(t)
        send_parts(t)
    for r in range(1, rounds):
        hid_t[r] = hid[r].T
    pool[...] = (block == lane_block).astype(jnp.bfloat16)

    multiply_last(1)
    early_over_z(2)
    early_over_z(3)

    for t in range(AHEAD, EARLY):
        multiply(t)

    def stage(work, item):
        @pl.when((item >= 0) & (item < items))
        def _():
            work(item)

    late = {2: ((multiply_last, 0),), items - 3: ((last_send_parts, 0),), items - 2: ((last_send_parts, 1),),
            items - 1: ((late_send_parts, 2), (late_send_parts, 3)),
            items: ((last_over_z, 0),), items + 1: ((last_over_z, 1), (last_encode, 2), (last_encode, 3)),
            items + 3: ((last_encode, 0), (last_encode, 1)),
            items + 5: ((last_update, 2), (last_update, 3), (last_update, 0), (last_update, 1))}

    @pl.loop(0, items + LAGS[-1])
    def _(t):
        stage(pass_on, t)
        stage(send_parts, t + AHEAD)
        stage(over_z, t - LAGS[0])
        for step, works in late.items():
            @pl.when(t == step)
            def _():
                for work, k in works:
                    work(k)
        stage(encode, t - LAGS[1])
        stage(update, t - LAGS[2])
        stage(multiply, t + EARLY)

    pltpu.make_async_copy(inbox, inbox, send_sem.at[0]).wait()
    pltpu.make_async_copy(last_inbox, last_inbox, send_sem.at[1]).wait()


def deliver(*refs):
    sem = refs[-1]
    arrays = (len(refs) - 1) // 2
    copies = []
    for i in range(arrays):
        half = refs[i].shape[1] // 2
        for j in range(2):
            piece = (0, pl.ds(j * half, half))
            copies.append(pltpu.make_async_copy(refs[i].at[piece], refs[arrays + i].at[piece], sem.at[i, j]))
    for copy in copies:
        copy.start()
    for copy in copies:
        copy.wait()


def per_device(params, public, mixed, hidden, cotangent):
    _, rows, width = params.shape
    _, rounds, tokens, rows_all = hidden.shape
    items = rounds * CHUNKS - 2
    w = width // CHUNKS
    piece = pltpu.VMEM((items, rows, w), jnp.bfloat16)
    state = pltpu.VMEM((CHUNKS, rows, w), jnp.float32)
    anywhere = pl.BlockSpec(memory_space=pl.ANY)
    in_vmem = pl.BlockSpec(memory_space=pltpu.VMEM)
    results = pl.pallas_call(
        kernel,
        out_shape=(pltpu.VMEM(params.shape, jnp.float32),) * 3,
        in_specs=[anywhere] * 5,
        out_specs=(in_vmem,) * 3,
        scratch_shapes=[
            pltpu.VMEM((rounds, tokens, rows_all), jnp.bfloat16),
            pltpu.VMEM((rounds, rows_all, tokens), jnp.bfloat16),
            pltpu.VMEM((items + 2, tokens, w), jnp.bfloat16),
            state, state, state,
            pltpu.VMEM((items, rows_all // rows, rows, w), jnp.bfloat16),
            pltpu.VMEM((items, INBOX, rows, w), jnp.bfloat16),
            *[piece] * 4,
            state, state,
            pltpu.VMEM((2 * LANES, LANES), jnp.bfloat16),
            pltpu.VMEM((PIECES, rows_all // rows, rows, w // 2), jnp.bfloat16),
            pltpu.VMEM((PIECES, INBOX, rows, w // 2), jnp.bfloat16),
            pltpu.VMEM((2, rows, w // 2), jnp.bfloat16),
            pltpu.VMEM((2, XSIDE - 1, rows, w // 2), jnp.bfloat16),
            pltpu.VMEM((PIECES, rows, w // 2), jnp.bfloat16),
            pltpu.SemaphoreType.DMA((5,)),
            pltpu.SemaphoreType.DMA((items + 2,)),
            pltpu.SemaphoreType.DMA((3, CHUNKS)),
            pltpu.SemaphoreType.DMA((2,)),
            pltpu.SemaphoreType.DMA((len(LANDS), items)),
            pltpu.SemaphoreType.DMA((len(LANDS), PIECES)),
        ],
        compiler_params=pltpu.CompilerParams(
            collective_id=0, has_side_effects=True, vmem_limit_bytes=40 * 1024 * 1024),
        cost_estimate=pl.CostEstimate(flops=340_000_000, bytes_accessed=5_000_000, transcendentals=0),
    )(*[pltpu.with_memory_space_constraint(a, pltpu.HBM) for a in (params, public, mixed, hidden, cotangent)])
    return pl.pallas_call(
        deliver,
        out_shape=(jax.ShapeDtypeStruct(params.shape, jnp.float32),) * 3,
        in_specs=[in_vmem] * 3,
        out_specs=(anywhere,) * 3,
        scratch_shapes=[pltpu.SemaphoreType.DMA((3, 2))],
        compiler_params=pltpu.CompilerParams(vmem_limit_bytes=1024 * 1024),
    )(*[pltpu.with_memory_space_constraint(a, pltpu.VMEM) for a in results])


def solution(mesh):
    state = P("blk", "fsdp", None)
    tokens = P("blk", None, "fsdp", None)
    return jax.shard_map(
        per_device,
        mesh=mesh,
        in_specs=(state, state, state, tokens, tokens),
        out_specs=(state, state, state),
        check_vma=False,
    )
```
